512 devices in a mesh: grp: 16 (over x, z_hi), pose: 32 (over y, z_lo, core).
Axes of the slice: x: 4, y: 4, z: 16 (z_hi: 4, z_lo: 4; z = z_hi * 4 + z_lo), core: 2. Of those that a mesh axis runs over, the one named last changes fastest.
Arguments:
- images: bfloat16 [2, 4096, 4096], P(None, 'grp')
- projections: bfloat16 [2, 4096, 4096], P(None, 'pose', 'grp')
- defocus: float32 [4096], P('grp')
- inv_sigma2: float32 [4096], replicated, may hold values from 0.005 to 0.05
- log_prior: float32 [64], replicated, may hold values from -4 to 4
- row_class: int32 [4096], P('pose'), may hold values from 0 to 63
- pose_block: int32 [4096], P('pose'), may hold values from 0 to 255, as said below
- significant: int32 [4096, 256], P('grp'), may hold values from 0 to 1, as said below
Outputs:
- posteriors: float32 [4096, 4096], P('grp', 'pose')
- back_proj: float32 [3, 4096, 4096], P(None, 'pose', 'grp')
The draws below stay inside these ranges and needn't reach their ends.
Inputs may be any that keep to these rules, and one draw needn't show every extreme that they name: `pose_block`: every block in 0 to 255 is the block of at least one row. Every particle has at least one significant block.
All inputs are finite; a program needn't handle non-finite values.
Results may differ from the reference program's by a relative error of at most 0.012.
Values may be sent and summed in bfloat16 or wider, within the bound.
No kernel may reach another device: no remote copies, remote signals or barrier semaphores. Data moves between devices by JAX's collectives and lax.ppermute only.
A program may use at most 128 MiB of HBM per device.

```python
import math
import jax
import jax.numpy as jnp
from jax import lax

PX = 4096
CLS = 64
PART_GRP = 256
NPART = 4096
ROWS = 4096
NBLK = 256
N_GRP = 16


def shared_fields(key):
    first, second = jax.random.split(key)
    proj_base = jax.random.normal(first, (2, ROWS, PX), jnp.float32)
    defocus_base = jnp.exp(jax.random.uniform(second, (NPART,), jnp.float32, math.log(20.0), math.log(60.0)))
    return (proj_base, defocus_base)


def drawn_rows(key):
    key = jax.random.fold_in(key, 11)
    particle = jnp.arange(NPART)
    offset = jax.random.randint(key, (), 0, ROWS)
    target = (particle * 37 + offset) % ROWS
    chosen = particle % 16 < 2
    return (target.astype(jnp.int32), chosen)


def draw_projections(key, part):
    proj_base, defocus_base = shared_fields(key)
    return proj_base.astype(jnp.bfloat16)


def draw_defocus(key, part):
    proj_base, defocus_base = shared_fields(key)
    return defocus_base


def draw_images(key, part):
    proj_base, defocus_base = shared_fields(key)
    target, chosen = drawn_rows(key)
    key = jax.random.fold_in(key, 3)
    first = jax.random.fold_in(key, 0)
    noise = jax.random.normal(first, (2, NPART, PX), jnp.float32)
    particle = jnp.arange(NPART)
    aligned = jnp.take(proj_base, target, axis=1)
    freq2 = (jnp.arange(PX, dtype=jnp.float32) + 0.5) / PX
    contrast = -jnp.sin(defocus_base[:, None] * freq2[None, :] + 0.1)
    level = (1 + particle // 16 % 4).astype(jnp.float32)
    strength = 0.5 + level * (6400.0 / PX)
    planted = strength[None, :, None] * contrast[None] * aligned + 0.3 * noise
    others = noise
    values = jnp.where(chosen[None, :, None], planted, others)
    return values.astype(jnp.bfloat16)


def draw_pose_block(key, part):
    key = jax.random.fold_in(key, 5)
    return (jax.random.permutation(key, ROWS) % NBLK).astype(jnp.int32)


def draw_significant(key, part):
    blocks = draw_pose_block(key, part)
    target, chosen = drawn_rows(key)
    key = jax.random.fold_in(key, 6)
    first, second = jax.random.split(key)
    chance = jax.random.randint(first, (NPART, NBLK), 0, 3) == 0
    forced = jax.random.randint(second, (NPART,), 0, NBLK)
    forced = jnp.where(chosen, jnp.take(blocks, target), forced)
    hit = jnp.arange(NBLK)[None, :] == forced[:, None]
    return jnp.logical_or(chance, hit).astype(jnp.int32)


def plant(result, rng, smallest, largest):
    extent = result.shape
    place = [jax.random.randint(jax.random.fold_in(rng, axis), (), 0, extent[axis]) for axis in range(len(extent))]
    result = result.at[tuple(place)].set(smallest)
    longest = extent.index(max(extent))
    place[longest] = (place[longest] + 1) % extent[longest]
    return result.at[tuple(place)].set(largest)


def normal_values(rng, dims, spread, bound, kind=jnp.bfloat16):
    entries = jax.random.normal(rng, dims, jnp.float32) * spread
    return jnp.minimum(jnp.maximum(entries, -bound), bound).astype(kind)


def setup_inputs(seed: int = 0) -> dict:
    splits = jax.random.split(jax.random.key(seed), 9)
    images = draw_images(jax.random.fold_in(splits[8], 71), 0)
    projections = draw_projections(jax.random.fold_in(splits[8], 71), 0)
    defocus = draw_defocus(jax.random.fold_in(splits[8], 71), 0)
    inv_sigma2 = jnp.clip(jnp.exp(jax.random.uniform(splits[3], (PX,), jnp.float32, math.log(0.005), math.log(0.05))), 0.005, 0.05)
    log_prior = normal_values(splits[4], (CLS,), 1.0, 4.0, jnp.float32)
    row_class = plant(jax.random.randint(splits[5], (ROWS,), 0, CLS), jax.random.fold_in(splits[5], 1), 0, CLS - 1).astype(jnp.int32)
    pose_block = draw_pose_block(jax.random.fold_in(splits[8], 71), 0)
    significant = draw_significant(jax.random.fold_in(splits[8], 71), 0)
    return dict(images=images, projections=projections, defocus=defocus, inv_sigma2=inv_sigma2, log_prior=log_prior, row_class=row_class, pose_block=pose_block, significant=significant)


def contrast_of(defocus):
    freq2 = (jnp.arange(PX, dtype=jnp.float32) + 0.5) / PX
    return -jnp.sin(defocus[:, None] * freq2[None, :] + 0.1)


def reference(images, projections, defocus, inv_sigma2, log_prior, row_class, pose_block, significant):
    contrast = contrast_of(defocus)
    weighted = (images.astype(jnp.float32) * (contrast * inv_sigma2[None, :])[None]).astype(jnp.bfloat16)
    contrast_noise = (contrast * contrast * inv_sigma2[None, :]).astype(jnp.bfloat16)
    proj_f = projections.astype(jnp.float32)
    proj_power = (proj_f[0] * proj_f[0] + proj_f[1] * proj_f[1]).astype(jnp.bfloat16)
    cross = jnp.einsum("cik,crk->ir", weighted.astype(jnp.float32), proj_f)
    power = jnp.dot(contrast_noise, proj_power.T, preferred_element_type=jnp.float32)
    prior_rows = log_prior[row_class]
    valid = jnp.take(significant, pose_block, axis=1) == 1
    scores = jnp.where(valid, cross - 0.5 * power + prior_rows[None, :], jnp.float32(-1e30))
    peak = jnp.max(scores, axis=1)
    shifted = jnp.exp(scores - peak[:, None])
    total = jnp.sum(shifted, axis=1)
    posteriors = shifted / total[:, None]
    post_bf = posteriors.astype(jnp.bfloat16)
    contrast_images = images.astype(jnp.float32) * contrast[None]
    stacked = jnp.concatenate([contrast_images, (contrast * contrast)[None]], axis=0).astype(jnp.bfloat16)
    groups_w = post_bf.reshape(N_GRP, PART_GRP, ROWS)
    groups_s = jnp.transpose(stacked.reshape(3, N_GRP, PART_GRP, PX), (1, 0, 2, 3))

    def add_group(carry, inputs):
        weights, slabs = inputs
        partial_sum = jnp.einsum("ir,cik->crk", weights.astype(jnp.float32), slabs.astype(jnp.float32))
        rounded = lax.optimization_barrier(partial_sum.astype(jnp.bfloat16))
        return carry + rounded.astype(jnp.float32), None

    back_proj, _ = lax.scan(add_group, jnp.zeros((3, ROWS, PX), jnp.float32), (groups_w, groups_s))
    return posteriors, back_proj
```

```python
import functools
import math

import jax
import jax.numpy as jnp
from jax import lax
from jax.experimental import pallas as pl
from jax.experimental.pallas import tpu as pltpu
from jax.sharding import PartitionSpec as P

NEG_FILL = -1e30
NX, NZH = 4, 4
NY, NZL, NC = 4, 4, 2
LANES = 128
TERM_ROWS = 16
VMEM_LIMIT = 20 << 20
MOST_VMEM = 63 << 20
SMALL_COST = pl.CostEstimate(flops=1, bytes_accessed=1, transcendentals=0)
INTERPRET = False


def grp_shift(dx):
    return [(x * NZH + z, ((x + dx) % NX) * NZH + z) for x in range(NX) for z in range(NZH)]


def pose_shift(dy, dz, dc):
    return [
        (
            (y * NZL + z) * NC + c,
            (((y + dy) % NY) * NZL + (z + dz) % NZL) * NC + (c + dc) % NC,
        )
        for y in range(NY)
        for z in range(NZL)
        for c in range(NC)
    ]


def share_pairs():
    n_pose = NY * NZL * NC
    pairs = []
    for x in range(NX):
        for zh in range(NZH):
            for y in range(NY):
                for zl in range(NZL):
                    for c in range(NC):
                        pose = (y * NZL + zl) * NC + c
                        src = x * NZH + zh
                        dst = ((x + y) % NX) * NZH + (zh + zl) % NZH
                        pairs.append((src * n_pose + pose, dst * n_pose + pose))
    return pairs


WEIGHT_ROWS = 32


def weight_kernel(images_ref, sin_ref, cos_ref, inv_ref, weighted_ref, noise_ref, token_ref):
    width = images_ref.shape[2]

    def body(i, _):
        rows = pl.ds(pl.multiple_of(i * WEIGHT_ROWS, WEIGHT_ROWS), WEIGHT_ROWS)
        sin_lo, cos_lo = sin_ref[rows, :LANES], cos_ref[rows, :LANES]
        sin_all, cos_all = sin_ref[rows, LANES:], cos_ref[rows, LANES:]
        for j in range(width // LANES):
            cols = slice(j * LANES, (j + 1) * LANES)
            contrast = -(sin_all[:, j : j + 1] * cos_lo + cos_all[:, j : j + 1] * sin_lo)
            scaled = contrast * inv_ref[:, cols]
            for c in range(2):
                image = images_ref[c, rows, cols].astype(jnp.float32)
                weighted_ref[c, rows, cols] = (image * scaled).astype(jnp.bfloat16)
            noise_ref[rows, cols] = (contrast * scaled).astype(jnp.bfloat16)
        return 0

    lax.fori_loop(0, images_ref.shape[1] // WEIGHT_ROWS, body, 0)
    token_ref[...] = jnp.zeros_like(token_ref)


def weight_images(images, defocus, inv_sigma2):
    _, n, width = images.shape
    low = jnp.arange(LANES, dtype=jnp.float32) / width
    high = (jnp.arange(LANES, dtype=jnp.float32) * LANES + 0.5) / width
    phase = jnp.concatenate(
        [defocus[:, None] * low[None, :], defocus[:, None] * high[None, :] + 0.1], axis=1
    )
    assert width <= LANES * LANES
    in_vmem = pl.BlockSpec(memory_space=pltpu.VMEM)
    return pl.pallas_call(
        weight_kernel,
        in_specs=[in_vmem] * 4,
        out_specs=[in_vmem] * 3,
        out_shape=[
            jax.ShapeDtypeStruct((2, n, width), jnp.bfloat16),
            jax.ShapeDtypeStruct((n, width), jnp.bfloat16),
            jax.ShapeDtypeStruct((8, LANES), jnp.float32),
        ],
        cost_estimate=SMALL_COST,
        compiler_params=pltpu.CompilerParams(vmem_limit_bytes=VMEM_LIMIT),
        interpret=INTERPRET,
        name="weight_images",
    )(images, jnp.sin(phase), jnp.cos(phase), inv_sigma2[None, :])


def dot_nt(a, b):
    return lax.dot_general(a, b, (((1,), (1,)), ((), ())), preferred_element_type=jnp.float32)


def score_kernel(
    proj_hbm, weighted_hbm, noise_hbm, bias_ref, _, scores_ref, log_sum_ref,
    proj_ref, weighted_ref, noise_ref, sems,
):
    n_x, n_z, _, _, slab = proj_ref.shape
    block = n_z * slab

    def copies(i):
        cols = slice(i * block, (i + 1) * block)
        return (
            pltpu.make_async_copy(proj_hbm.at[i], proj_ref.at[i], sems.at[0, i]),
            pltpu.make_async_copy(
                weighted_hbm.at[:, :, cols], weighted_ref.at[:, :, cols], sems.at[1, i]
            ),
            pltpu.make_async_copy(noise_hbm.at[:, cols], noise_ref.at[:, cols], sems.at[2, i]),
        )

    for i in range(n_x):
        for copy in copies(i):
            copy.start()
    total = jnp.zeros(scores_ref.shape, jnp.float32)
    half_power = jnp.zeros(scores_ref.shape, jnp.float32)
    for i in range(n_x):
        for copy in copies(i):
            copy.wait()
        for z in range(n_z):
            cols = slice(i * block + z * slab, i * block + (z + 1) * slab)
            real, imag = proj_ref[i, z, 0], proj_ref[i, z, 1]
            real_f, imag_f = real.astype(jnp.float32), imag.astype(jnp.float32)
            power = (real_f * real_f + imag_f * imag_f).astype(jnp.bfloat16)
            total += dot_nt(real, weighted_ref[0, :, cols])
            total += dot_nt(imag, weighted_ref[1, :, cols])
            half_power += dot_nt(power, noise_ref[:, cols])
    bias = bias_ref[...]
    scores = jnp.where(bias == NEG_FILL, bias, total - 0.5 * half_power + bias)
    scores_ref[...] = scores
    peak = jnp.max(scores, axis=0, keepdims=True)
    log_sum = peak + jnp.log(jnp.sum(jnp.exp(scores - peak), axis=0, keepdims=True))
    log_sum_ref[...] = jnp.broadcast_to(log_sum[None], log_sum_ref.shape)


def score(proj, weighted, noise, bias, token, copies):
    n_x, rows = proj.shape[0], proj.shape[3]
    n = weighted.shape[1]
    in_hbm, in_vmem = pl.BlockSpec(memory_space=pl.ANY), pl.BlockSpec(memory_space=pltpu.VMEM)
    return pl.pallas_call(
        score_kernel,
        in_specs=[in_hbm] * 3 + [in_vmem] * 2,
        out_specs=[pl.BlockSpec(), in_vmem],
        out_shape=[
            jax.ShapeDtypeStruct((rows, n), jnp.float32),
            jax.ShapeDtypeStruct((copies, 1, n), jnp.float32),
        ],
        scratch_shapes=[
            pltpu.VMEM(proj.shape, jnp.bfloat16),
            pltpu.VMEM(weighted.shape, jnp.bfloat16),
            pltpu.VMEM(noise.shape, jnp.bfloat16),
            pltpu.SemaphoreType.DMA((3, n_x)),
        ],
        cost_estimate=SMALL_COST,
        compiler_params=pltpu.CompilerParams(vmem_limit_bytes=MOST_VMEM),
        interpret=INTERPRET,
        name="score",
    )(proj, weighted, noise, bias, token)


def posterior_kernel(core_ref, scores_ref, log_sums_ref, post_ref, post_bf_ref):
    parts = log_sums_ref[...]
    peak = jnp.max(parts, axis=0)
    log_sum = peak + jnp.log(jnp.sum(jnp.exp(parts - peak[None]), axis=0))
    posteriors = jnp.exp(scores_ref[...] - log_sum)
    half = posteriors.shape[1] // NC
    swapped = jnp.concatenate([posteriors[:, half:], posteriors[:, :half]], axis=1)
    own_first = jnp.where(core_ref[0] == 0, posteriors, swapped).astype(jnp.bfloat16)
    post_bf_ref[...] = own_first
    post_ref[...] = posteriors.T


def posterior(core, scores, log_sums):
    rows, n = scores.shape
    return pl.pallas_call(
        posterior_kernel,
        in_specs=[
            pl.BlockSpec(memory_space=pltpu.SMEM),
            pl.BlockSpec(),
            pl.BlockSpec(memory_space=pltpu.VMEM),
        ],
        out_shape=[
            jax.ShapeDtypeStruct((n, rows), jnp.float32),
            jax.ShapeDtypeStruct((rows, n), jnp.bfloat16),
        ],
        cost_estimate=SMALL_COST,
        compiler_params=pltpu.CompilerParams(vmem_limit_bytes=VMEM_LIMIT),
        interpret=INTERPRET,
        name="posterior",
    )(core[None], scores, log_sums)


SIN_TERMS = tuple(
    (-1) ** n * (2 * math.pi) ** (2 * n + 1) / math.factorial(2 * n + 1) for n in range(7)
)


def squared_contrast(defocus, start, pixels, width):
    pixel = start + lax.broadcasted_iota(jnp.int32, (pixels, defocus.shape[1]), 0)
    freq2 = (pixel.astype(jnp.float32) + 0.5) * (1.0 / width)
    turns = (freq2 * defocus + 0.1) * (1.0 / math.pi)
    turns = 0.25 - jnp.abs(turns - jnp.round(turns))
    square = turns * turns
    value = jnp.full_like(square, SIN_TERMS[-1])
    for term in SIN_TERMS[-2::-1]:
        value = value * square + term
    return 0.5 - 0.5 * (value * turns)


def defocus_terms(defocus):
    scaled = defocus * (1.0 / 256.0)
    first = lax.reduce_precision(scaled, 8, 7)
    second = lax.reduce_precision(scaled - first, 8, 7)
    third = scaled - first - second
    return jnp.stack([first, second, third]).astype(jnp.bfloat16)


def back_kernel(sources, added, width, start_ref, *refs):
    n_s = len(sources)
    hbm, before_ref = refs[: n_s + 2], refs[n_s + 2] if added else None
    out_ref, post_ref, own_ref, other_ref, sems = refs[n_s + 2 + added :]
    slab = out_ref.shape[2]
    half = post_ref.shape[3] // NC

    def copies(i):
        pairs = [(src.at[sources[i]], dst.at[i]) for src, dst in zip(hbm[n_s:], (own_ref, other_ref))]
        pairs.append((hbm[i], post_ref.at[i]))
        return [
            pltpu.make_async_copy(src, dst, sems.at[i, j]) for j, (src, dst) in enumerate(pairs)
        ]

    for i in range(n_s):
        for copy in copies(i):
            copy.start()
    if added:
        sums = [before_ref[c] for c in range(3)]
    else:
        sums = [jnp.zeros(out_ref.shape[1:], jnp.float32) for _ in range(3)]
    for i in range(n_s):
        for copy in copies(i):
            copy.wait()
        for t in range(post_ref.shape[1]):
            for stack, at in ((own_ref, 0), (other_ref, half)):
                post = post_ref[i, t, :, at : at + half]
                for c in range(2):
                    image = stack[i, t, c * half : (c + 1) * half]
                    sums[c] += jnp.dot(post, image, preferred_element_type=jnp.float32)
                terms = stack[i, t, NC * half : NC * half + TERM_ROWS].astype(jnp.float32)
                defocus = (terms[0:1, :half] + terms[1:2, :half] + terms[2:3, :half]) * 256.0
                square = squared_contrast(defocus, start_ref[0], slab, width)
                sums[2] += dot_nt(post, square.astype(jnp.bfloat16))
    for c in range(3):
        out_ref[c] = sums[c]


def back_project(start, width, sources, posts, stacks, before=None):
    n_s, (n_z, rows, n) = len(sources), posts[0].shape
    slab = stacks[0].shape[3]
    in_hbm, in_vmem = pl.BlockSpec(memory_space=pl.ANY), pl.BlockSpec(memory_space=pltpu.VMEM)
    added = before is not None
    scratch = [pltpu.VMEM((n_s, n_z, rows, n), jnp.bfloat16)]
    scratch += [pltpu.VMEM((n_s,) + stack.shape[1:], jnp.bfloat16) for stack in stacks]
    return pl.pallas_call(
        functools.partial(back_kernel, sources, added, width),
        in_specs=[pl.BlockSpec(memory_space=pltpu.SMEM)]
        + [in_hbm] * (n_s + 2)
        + [in_vmem] * added,
        out_specs=in_vmem,
        out_shape=jax.ShapeDtypeStruct((3, rows, slab), jnp.float32),
        scratch_shapes=scratch + [pltpu.SemaphoreType.DMA((n_s, 3))],
        cost_estimate=SMALL_COST,
        compiler_params=pltpu.CompilerParams(vmem_limit_bytes=MOST_VMEM),
        interpret=INTERPRET,
        name="back_project",
    )(start[None], *posts, *stacks, *([before] if added else []))


def exchange(copies, axis, groups=None):
    return lax.all_to_all(copies, axis, 0, 0, axis_index_groups=groups)


def copies_of(value, size):
    return jnp.broadcast_to(value[None], (size,) + value.shape)


def on_device(
    images, projections, defocus, inv_sigma2, log_prior, row_class, pose_block, significant
):
    _, n, width = images.shape
    _, rows, slab = projections.shape
    half = n // NC
    group, pose = lax.axis_index("grp"), lax.axis_index("pose")
    x, zh = group >> 2, group & 3
    y, zl, core = pose >> 3, (pose >> 1) & 3, pose & 1

    z_groups = [[a * NZH + b for b in range(NZH)] for a in range(NX)]
    x_groups = [[a * NZH + b for a in range(NX)] for b in range(NZH)]
    y_groups = [
        [(a * NZL + b) * NC + c for a in range(NY)] for b in range(NZL) for c in range(NC)
    ]
    with jax.named_scope("gather_projections"):
        proj_z = lax.all_gather(projections, "grp", axis=0, axis_index_groups=z_groups)
        proj_z, defocus = lax.optimization_barrier((proj_z, defocus))
        proj = lax.all_gather(proj_z, "grp", axis=0, axis_index_groups=x_groups)

    with jax.named_scope("exchange_images"):
        target = (((x + y) & 3) << 2) + ((zh + zl) & 3)
        part = lax.dynamic_slice(images, (0, core * half, target * slab), (2, half, slab))
        part_defocus = lax.dynamic_slice(defocus, (core * half,), (half,))
        pixel = (target * slab + jnp.arange(slab)).astype(jnp.float32)
        contrast = -jnp.sin(part_defocus[:, None] * ((pixel + 0.5) / width)[None, :] + 0.1)
        part = (part.astype(jnp.float32) * contrast[None]).astype(jnp.bfloat16)
        terms = jnp.pad(defocus_terms(part_defocus), ((0, TERM_ROWS - 3), (0, slab - half)))
        share = jnp.concatenate([part.reshape(2 * half, slab), terms], axis=0)
        share = lax.ppermute(share, ("grp", "pose"), share_pairs())

    with jax.named_scope("weights"):
        weighted, noise, token = weight_images(images, defocus, inv_sigma2)
        class_match = row_class[:, None] == jnp.arange(log_prior.shape[0])[None, :]
        prior_rows = jnp.sum(jnp.where(class_match, log_prior[None, :], 0.0), axis=1)
        block_table = pose_block[:, None] == jnp.arange(significant.shape[1])[None, :]
        hits = jnp.einsum(
            "rb,ib->ri",
            block_table.astype(jnp.bfloat16),
            significant.astype(jnp.bfloat16),
            preferred_element_type=jnp.float32,
        )
        bias = jnp.where(hits > 0.5, prior_rows[:, None], jnp.float32(NEG_FILL))

    with jax.named_scope("gather_images"):
        share, token, bias = lax.optimization_barrier((share, token, bias))
        turned = copies_of(share, NZL)
        for d in (1, 2, 3):
            block = lax.ppermute(share, "pose", pose_shift(0, d, 0))
            turned = lax.dynamic_update_slice_in_dim(turned, block[None], (zh - zl + d) & 3, 0)
        turned, proj = lax.optimization_barrier((turned, proj))
        own = lax.all_gather(turned, "pose", axis=0, axis_index_groups=y_groups)

    with jax.named_scope("scores"):
        scores, log_sum = score(proj, weighted, noise, bias, token, NY * NZL * NC)

    with jax.named_scope("softmax"):
        posteriors, post_bf = posterior(core, scores, exchange(log_sum, "pose"))

    with jax.named_scope("gather_posteriors"):
        post = [lax.all_gather(post_bf, "grp", axis=0, axis_index_groups=z_groups)] + [None] * 3
        for d in (2, 1, 3):
            post[d] = lax.ppermute(post[0], "grp", grp_shift(d))
        post[0], own = lax.optimization_barrier((post[0], own))
        other = lax.ppermute(own, "pose", pose_shift(0, 0, 1))

    with jax.named_scope("back_project"):
        start, stacks = group * slab, (own, other)
        back_proj = back_project(start, width, (0, 1), post[:2], stacks)
        back_proj = back_project(start, width, (3, 2), (post[3], post[2]), stacks, back_proj)
    return (posteriors, back_proj)


def solution(mesh):
    placed = (
        P(None, "grp", None),
        P(None, "pose", "grp"),
        P("grp"),
        P(),
        P(),
        P("pose"),
        P("pose"),
        P("grp", None),
    )
    return jax.shard_map(
        on_device,
        mesh=mesh,
        in_specs=placed,
        out_specs=(P("grp", "pose"), P(None, "pose", "grp")),
        check_vma=False,
    )
```

```python
import functools
import math

import jax
import jax.numpy as jnp
from jax import lax
from jax.experimental import pallas as pl
from jax.experimental.pallas import tpu as pltpu
from jax.sharding import PartitionSpec as P

NEG_FILL = -1e30
NX, NZH = 4, 4
NY, NZL, NC = 4, 4, 2
LANES = 128
TERM_ROWS = 16
VMEM_LIMIT = 20 << 20
MOST_VMEM = 63 << 20
BACK_VMEM = 52 << 20
SMALL_COST = pl.CostEstimate(flops=1, bytes_accessed=1, transcendentals=0)
INTERPRET = False


def grp_shift(dx):
    return [(x * NZH + z, ((x + dx) % NX) * NZH + z) for x in range(NX) for z in range(NZH)]


def pose_shift(dy, dz, dc):
    return [
        (
            (y * NZL + z) * NC + c,
            (((y + dy) % NY) * NZL + (z + dz) % NZL) * NC + (c + dc) % NC,
        )
        for y in range(NY)
        for z in range(NZL)
        for c in range(NC)
    ]


def share_pairs():
    n_pose = NY * NZL * NC
    pairs = []
    for x in range(NX):
        for zh in range(NZH):
            for y in range(NY):
                for zl in range(NZL):
                    for c in range(NC):
                        pose = (y * NZL + zl) * NC + c
                        src = x * NZH + zh
                        dst = ((x + y) % NX) * NZH + (zh + zl) % NZH
                        pairs.append((src * n_pose + pose, dst * n_pose + pose))
    return pairs


SIN_TERMS = tuple(
    (-1) ** n * (2 * math.pi) ** (2 * n + 1) / math.factorial(2 * n + 1) for n in range(7)
)


def sin_quarter(t, scale=1.0):
    square = t * t
    value = square * (scale * SIN_TERMS[-1]) + scale * SIN_TERMS[-2]
    for term in SIN_TERMS[-3::-1]:
        value = value * square + scale * term
    return value * t


WEIGHT_ROWS = 32


def dot_nt(a, b):
    return lax.dot_general(a, b, (((1,), (1,)), ((), ())), preferred_element_type=jnp.float32)


def score_terms(proj, weighted_real, weighted_imag, noise):
    n_z = proj.shape[0]
    real = jnp.concatenate([proj[z, 0] for z in range(n_z)], axis=1)
    imag = jnp.concatenate([proj[z, 1] for z in range(n_z)], axis=1)
    real_f, imag_f = real.astype(jnp.float32), imag.astype(jnp.float32)
    power = (real_f * real_f + imag_f * imag_f).astype(jnp.bfloat16)
    return dot_nt(real, weighted_real) + dot_nt(imag, weighted_imag) - 0.5 * dot_nt(power, noise)


def weight_kernel(
    x_ref, images_ref, sin_ref, cos_ref, inv_ref, proj_ref, weighted_ref, noise_ref, part_ref
):
    width = images_ref.shape[2]

    def body(i, _):
        rows = pl.ds(pl.multiple_of(i * WEIGHT_ROWS, WEIGHT_ROWS), WEIGHT_ROWS)
        sin_lo, cos_lo = sin_ref[rows, :LANES], cos_ref[rows, :LANES]
        sin_all, cos_all = sin_ref[rows, LANES:], cos_ref[rows, LANES:]
        for j in range(width // LANES):
            cols = slice(j * LANES, (j + 1) * LANES)
            contrast = -(sin_all[:, j : j + 1] * cos_lo + cos_all[:, j : j + 1] * sin_lo)
            scaled = contrast * inv_ref[:, cols]
            for c in range(2):
                image = images_ref[c, rows, cols].astype(jnp.float32)
                weighted_ref[c, rows, cols] = (image * scaled).astype(jnp.bfloat16)
            noise_ref[rows, cols] = (contrast * scaled).astype(jnp.bfloat16)
        return 0

    lax.fori_loop(0, images_ref.shape[1] // WEIGHT_ROWS, body, 0)
    block = proj_ref.shape[0] * proj_ref.shape[3]
    cols = pl.ds(pl.multiple_of(x_ref[0] * block, block), block)
    part_ref[...] = score_terms(
        proj_ref, weighted_ref[0, :, cols], weighted_ref[1, :, cols], noise_ref[:, cols]
    )


def weight_images(x, images, defocus, inv_sigma2, proj):
    _, n, width = images.shape
    low = jnp.arange(LANES, dtype=jnp.float32) / width
    high = (jnp.arange(LANES, dtype=jnp.float32) * LANES + 0.5) / width
    phase = jnp.concatenate(
        [defocus[:, None] * low[None, :], defocus[:, None] * high[None, :] + 0.1], axis=1
    )
    assert width <= LANES * LANES
    in_vmem = pl.BlockSpec(memory_space=pltpu.VMEM)
    return pl.pallas_call(
        weight_kernel,
        in_specs=[pl.BlockSpec(memory_space=pltpu.SMEM)] + [in_vmem] * 5,
        out_specs=[in_vmem] * 3,
        out_shape=[
            jax.ShapeDtypeStruct((2, n, width), jnp.bfloat16),
            jax.ShapeDtypeStruct((n, width), jnp.bfloat16),
            jax.ShapeDtypeStruct((proj.shape[2], n), jnp.float32),
        ],
        cost_estimate=SMALL_COST,
        compiler_params=pltpu.CompilerParams(vmem_limit_bytes=VMEM_LIMIT),
        interpret=INTERPRET,
        name="weight_images",
    )(x[None], images, jnp.sin(phase), jnp.cos(phase), inv_sigma2[None, :], proj)


def score_kernel(
    x_ref, proj_hbm, weighted_hbm, noise_hbm, part_ref, bias_ref, scores_ref, log_sum_ref,
    proj_ref, weighted_ref, noise_ref, sems,
):
    n_s, n_z, _, _, slab = proj_ref.shape
    block = n_z * slab

    def copies(i):
        source = (x_ref[0] + i + 1) & (NX - 1)
        cols = pl.ds(pl.multiple_of(source * block, block), block)
        return (
            pltpu.make_async_copy(proj_hbm.at[source], proj_ref.at[i], sems.at[0, i]),
            pltpu.make_async_copy(weighted_hbm.at[:, :, cols], weighted_ref.at[i], sems.at[1, i]),
            pltpu.make_async_copy(noise_hbm.at[:, cols], noise_ref.at[i], sems.at[2, i]),
        )

    for i in range(n_s):
        for copy in copies(i):
            copy.start()
    total = part_ref[...]
    for i in range(n_s):
        for copy in copies(i):
            copy.wait()
        total += score_terms(proj_ref.at[i], weighted_ref[i, 0], weighted_ref[i, 1], noise_ref[i])
    bias = bias_ref[...]
    scores = jnp.where(bias == NEG_FILL, bias, total + bias)
    scores_ref[...] = scores
    peak = jnp.max(scores, axis=0, keepdims=True)
    log_sum = peak + jnp.log(jnp.sum(jnp.exp(scores - peak), axis=0, keepdims=True))
    log_sum_ref[...] = jnp.broadcast_to(log_sum[None], log_sum_ref.shape)


def score(x, proj, weighted, noise, part, bias, copies):
    n_x, n_z, _, rows, slab = proj.shape
    n = weighted.shape[1]
    in_hbm, in_vmem = pl.BlockSpec(memory_space=pl.ANY), pl.BlockSpec(memory_space=pltpu.VMEM)
    return pl.pallas_call(
        score_kernel,
        in_specs=[pl.BlockSpec(memory_space=pltpu.SMEM)] + [in_hbm] * 3 + [in_vmem] * 2,
        out_specs=[in_vmem] * 2,
        out_shape=[
            jax.ShapeDtypeStruct((rows, n), jnp.float32),
            jax.ShapeDtypeStruct((copies, 1, n), jnp.float32),
        ],
        scratch_shapes=[
            pltpu.VMEM((n_x - 1,) + proj.shape[1:], jnp.bfloat16),
            pltpu.VMEM((n_x - 1, 2, n, n_z * slab), jnp.bfloat16),
            pltpu.VMEM((n_x - 1, n, n_z * slab), jnp.bfloat16),
            pltpu.SemaphoreType.DMA((3, n_x - 1)),
        ],
        cost_estimate=SMALL_COST,
        compiler_params=pltpu.CompilerParams(vmem_limit_bytes=MOST_VMEM),
        interpret=INTERPRET,
        name="score",
    )(x[None], proj, weighted, noise, part, bias)


def posterior_kernel(core_ref, scores_ref, log_sums_ref, post_ref, post_bf_ref):
    parts = log_sums_ref[...]
    peak = jnp.max(parts, axis=0)
    log_sum = peak + jnp.log(jnp.sum(jnp.exp(parts - peak[None]), axis=0))
    posteriors = jnp.exp(scores_ref[...] - log_sum)
    half = posteriors.shape[1] // NC
    swapped = jnp.concatenate([posteriors[:, half:], posteriors[:, :half]], axis=1)
    own_first = jnp.where(core_ref[0] == 0, posteriors, swapped).astype(jnp.bfloat16)
    post_bf_ref[...] = own_first
    post_ref[...] = posteriors.T


def posterior(core, scores, log_sums):
    rows, n = scores.shape
    return pl.pallas_call(
        posterior_kernel,
        in_specs=[
            pl.BlockSpec(memory_space=pltpu.SMEM),
            pl.BlockSpec(),
            pl.BlockSpec(memory_space=pltpu.VMEM),
        ],
        out_shape=[
            jax.ShapeDtypeStruct((n, rows), jnp.float32),
            jax.ShapeDtypeStruct((rows, n), jnp.bfloat16),
        ],
        cost_estimate=SMALL_COST,
        compiler_params=pltpu.CompilerParams(vmem_limit_bytes=VMEM_LIMIT),
        interpret=INTERPRET,
        name="posterior",
    )(core[None], scores, log_sums)


def squared_contrast(defocus, freq2):
    turns = freq2 * (defocus * (1.0 / math.pi)) + 0.1 / math.pi
    return 0.5 - sin_quarter(0.25 - jnp.abs(turns - jnp.round(turns)), 0.5)


def defocus_terms(defocus):
    scaled = defocus * (1.0 / 256.0)
    first = lax.reduce_precision(scaled, 8, 7)
    second = lax.reduce_precision(scaled - first, 8, 7)
    third = scaled - first - second
    return jnp.stack([first, second, third]).astype(jnp.bfloat16)


def back_kernel(sources, added, width, start_ref, *refs):
    n_s = len(sources)
    posts, hbm = refs[:n_s], refs[n_s : n_s + 2]
    before_ref = refs[n_s + 2] if added else None
    out_ref, own_ref, other_ref, sems = refs[n_s + 2 + added :]
    n_z, _, n = posts[0].shape
    slab, half = out_ref.shape[2], n // NC

    def copies(i):
        pairs = zip(hbm, (own_ref, other_ref))
        return [
            pltpu.make_async_copy(src.at[sources[i]], dst.at[i], sems.at[i, j])
            for j, (src, dst) in enumerate(pairs)
        ]

    for i in range(n_s):
        for copy in copies(i):
            copy.start()
    pixel = start_ref[0] + lax.broadcasted_iota(jnp.int32, (slab, half), 0)
    freq2 = (pixel.astype(jnp.float32) + 0.5) * (1.0 / width)
    for i in range(n_s):
        for copy in copies(i):
            copy.wait()
        stacks = [stack[i, t] for t in range(n_z) for stack in (own_ref, other_ref)]
        post = jnp.concatenate([posts[i][t] for t in range(n_z)], axis=1)
        first = added or i > 0
        for c in range(2):
            images = jnp.concatenate([stack[c * half : (c + 1) * half] for stack in stacks], axis=0)
            total = jnp.dot(post, images, preferred_element_type=jnp.float32)
            before = (out_ref if i > 0 else before_ref)[c] if first else None
            out_ref[c] = total + before if first else total
        squares = []
        for stack in stacks:
            terms = stack[NC * half : NC * half + TERM_ROWS].astype(jnp.float32)
            defocus = (terms[0:1, :half] + terms[1:2, :half] + terms[2:3, :half]) * 256.0
            squares.append(squared_contrast(defocus, freq2).astype(jnp.bfloat16))
        total = dot_nt(post, jnp.concatenate(squares, axis=1))
        before = (out_ref if i > 0 else before_ref)[2] if first else None
        out_ref[2] = total + before if first else total


def back_project(start, width, sources, posts, stacks, before=None):
    n_s, rows = len(sources), posts[0].shape[1]
    slab = stacks[0].shape[3]
    in_hbm, in_vmem = pl.BlockSpec(memory_space=pl.ANY), pl.BlockSpec(memory_space=pltpu.VMEM)
    added = before is not None
    scratch = [pltpu.VMEM((n_s,) + stack.shape[1:], jnp.bfloat16) for stack in stacks]
    return pl.pallas_call(
        functools.partial(back_kernel, sources, added, width),
        in_specs=[pl.BlockSpec(memory_space=pltpu.SMEM)]
        + [in_vmem] * n_s
        + [in_hbm] * 2
        + [in_vmem] * added,
        out_specs=in_vmem,
        out_shape=jax.ShapeDtypeStruct((3, rows, slab), jnp.float32),
        scratch_shapes=scratch + [pltpu.SemaphoreType.DMA((n_s, 2))],
        cost_estimate=SMALL_COST,
        compiler_params=pltpu.CompilerParams(vmem_limit_bytes=BACK_VMEM),
        interpret=INTERPRET,
        name="back_project",
    )(start[None], *posts, *stacks, *([before] if added else []))


def exchange(copies, axis, groups=None):
    return lax.all_to_all(copies, axis, 0, 0, axis_index_groups=groups)


def copies_of(value, size):
    return jnp.broadcast_to(value[None], (size,) + value.shape)


def on_device(
    images, projections, defocus, inv_sigma2, log_prior, row_class, pose_block, significant
):
    _, n, width = images.shape
    _, rows, slab = projections.shape
    half = n // NC
    group, pose = lax.axis_index("grp"), lax.axis_index("pose")
    x, zh = group >> 2, group & 3
    y, zl, core = pose >> 3, (pose >> 1) & 3, pose & 1

    z_groups = [[a * NZH + b for b in range(NZH)] for a in range(NX)]
    x_groups = [[a * NZH + b for a in range(NX)] for b in range(NZH)]
    y_groups = [
        [(a * NZL + b) * NC + c for a in range(NY)] for b in range(NZL) for c in range(NC)
    ]
    with jax.named_scope("gather_projections"):
        proj_z = lax.all_gather(projections, "grp", axis=0, axis_index_groups=z_groups)
        proj_z, defocus = lax.optimization_barrier((proj_z, defocus))
        proj = lax.all_gather(proj_z, "grp", axis=0, axis_index_groups=x_groups)

    with jax.named_scope("exchange_images"):
        target = (((x + y) & 3) << 2) + ((zh + zl) & 3)
        cut = lax.dynamic_slice(images, (0, core * half, target * slab), (2, half, slab))
        part_defocus = lax.dynamic_slice(defocus, (core * half,), (half,))
        pixel = (target * slab + jnp.arange(slab)).astype(jnp.float32)
        contrast = -jnp.sin(part_defocus[:, None] * ((pixel + 0.5) / width)[None, :] + 0.1)
        cut = (cut.astype(jnp.float32) * contrast[None]).astype(jnp.bfloat16)
        terms = jnp.pad(defocus_terms(part_defocus), ((0, TERM_ROWS - 3), (0, slab - half)))
        share = jnp.concatenate([cut.reshape(2 * half, slab), terms], axis=0)
        share = lax.ppermute(share, ("grp", "pose"), share_pairs())

    with jax.named_scope("weights"):
        weighted, noise, part = weight_images(x, images, defocus, inv_sigma2, proj_z)
        class_match = row_class[:, None] == jnp.arange(log_prior.shape[0])[None, :]
        prior_rows = jnp.sum(jnp.where(class_match, log_prior[None, :], 0.0), axis=1)
        block_table = pose_block[:, None] == jnp.arange(significant.shape[1])[None, :]
        hits = jnp.einsum(
            "rb,ib->ri",
            block_table.astype(jnp.bfloat16),
            significant.astype(jnp.bfloat16),
            preferred_element_type=jnp.float32,
        )
        bias = jnp.where(hits > 0.5, prior_rows[:, None], jnp.float32(NEG_FILL))

    with jax.named_scope("gather_images"):
        share, part, bias = lax.optimization_barrier((share, part, bias))
        turned = copies_of(share, NZL)
        for d in (1, 2, 3):
            block = lax.ppermute(share, "pose", pose_shift(0, d, 0))
            turned = lax.dynamic_update_slice_in_dim(turned, block[None], (zh - zl + d) & 3, 0)
        turned, proj = lax.optimization_barrier((turned, proj))
        own = lax.all_gather(turned, "pose", axis=0, axis_index_groups=y_groups)

    with jax.named_scope("scores"):
        scores, log_sum = score(x, proj, weighted, noise, part, bias, NY * NZL * NC)

    with jax.named_scope("softmax"):
        posteriors, post_bf = posterior(core, scores, exchange(log_sum, "pose"))

    with jax.named_scope("gather_posteriors"):
        post = [lax.all_gather(post_bf, "grp", axis=0, axis_index_groups=z_groups)] + [None] * 3
        for d in (1, 3, 2):
            post[d] = lax.ppermute(post[0], "grp", grp_shift(d))
        post[0], own = lax.optimization_barrier((post[0], own))
        other = lax.ppermute(own, "pose", pose_shift(0, 0, 1))

    with jax.named_scope("back_project"):
        start, stacks = group * slab, (own, other)
        back_proj = back_project(start, width, (0, 1), post[:2], stacks)
        back_proj = back_project(start, width, (3, 2), (post[3], post[2]), stacks, back_proj)
    return (posteriors, back_proj)


def solution(mesh):
    placed = (
        P(None, "grp", None),
        P(None, "pose", "grp"),
        P("grp"),
        P(),
        P(),
        P("pose"),
        P("pose"),
        P("grp", None),
    )
    return jax.shard_map(
        on_device,
        mesh=mesh,
        in_specs=placed,
        out_specs=(P("grp", "pose"), P(None, "pose", "grp")),
        check_vma=False,
    )
```

```python
import functools
import math

import jax
import jax.numpy as jnp
from jax import lax
from jax.experimental import pallas as pl
from jax.experimental.pallas import tpu as pltpu
from jax.sharding import PartitionSpec as P

NEG_FILL = -1e30
NX, NZH = 4, 4
NY, NZL, NC = 4, 4, 2
LANES = 128
TERM_ROWS = 16
VMEM_LIMIT = 20 << 20
MOST_VMEM = 63 << 20
BACK_VMEM = 52 << 20
WEIGHT_VMEM = 60 << 20
SMALL_COST = pl.CostEstimate(flops=1, bytes_accessed=1, transcendentals=0)
INTERPRET = False


def grp_shift(dx):
    return [(x * NZH + z, ((x + dx) % NX) * NZH + z) for x in range(NX) for z in range(NZH)]


def pose_shift(dy, dz, dc):
    return [
        (
            (y * NZL + z) * NC + c,
            (((y + dy) % NY) * NZL + (z + dz) % NZL) * NC + (c + dc) % NC,
        )
        for y in range(NY)
        for z in range(NZL)
        for c in range(NC)
    ]


def share_pairs():
    n_pose = NY * NZL * NC
    pairs = []
    for x in range(NX):
        for zh in range(NZH):
            for y in range(NY):
                for zl in range(NZL):
                    for c in range(NC):
                        pose = (y * NZL + zl) * NC + c
                        src = x * NZH + zh
                        dst = ((x + y) % NX) * NZH + (zh + zl) % NZH
                        pairs.append((src * n_pose + pose, dst * n_pose + pose))
    return pairs


SIN_TERMS = tuple(
    (-1) ** n * (2 * math.pi) ** (2 * n + 1) / math.factorial(2 * n + 1) for n in range(7)
)


def sin_quarter(t, scale=1.0):
    square = t * t
    value = square * (scale * SIN_TERMS[-1]) + scale * SIN_TERMS[-2]
    for term in SIN_TERMS[-3::-1]:
        value = value * square + scale * term
    return value * t


WEIGHT_ROWS = 32


def dot_nt(a, b):
    return lax.dot_general(a, b, (((1,), (1,)), ((), ())), preferred_element_type=jnp.float32)


def score_terms(proj, weighted_real, weighted_imag, noise):
    n_z = proj.shape[0]
    real = jnp.concatenate([proj[z, 0] for z in range(n_z)], axis=1)
    imag = jnp.concatenate([proj[z, 1] for z in range(n_z)], axis=1)
    real_f, imag_f = real.astype(jnp.float32), imag.astype(jnp.float32)
    power = (real_f * real_f + imag_f * imag_f).astype(jnp.bfloat16)
    return dot_nt(real, weighted_real) + dot_nt(imag, weighted_imag) - 0.5 * dot_nt(power, noise)


def weight_kernel(
    x_ref, images_hbm, sin_ref, cos_ref, inv_ref, proj_ref, weighted_hbm, noise_hbm, part_ref,
    images_ref, weighted_ref, noise_ref, sems,
):
    n, width = images_ref.shape[1:]
    steps = n // WEIGHT_ROWS

    def rows_of(i):
        return pl.ds(pl.multiple_of(i * WEIGHT_ROWS, WEIGHT_ROWS), WEIGHT_ROWS)

    def copy_in(i):
        rows = rows_of(i)
        return pltpu.make_async_copy(
            images_hbm.at[:, rows, :], images_ref.at[:, rows, :], sems.at[0, i]
        )

    def copies_out(i):
        rows = rows_of(i)
        return (
            pltpu.make_async_copy(
                weighted_ref.at[:, rows, :], weighted_hbm.at[:, rows, :], sems.at[1, i]
            ),
            pltpu.make_async_copy(noise_ref.at[rows, :], noise_hbm.at[rows, :], sems.at[2, i]),
        )

    def start(i, _):
        copy_in(i).start()
        return 0

    def body(i, _):
        copy_in(i).wait()
        rows = rows_of(i)
        sin_lo, cos_lo = sin_ref[rows, :LANES], cos_ref[rows, :LANES]
        sin_all, cos_all = sin_ref[rows, LANES:], cos_ref[rows, LANES:]
        for j in range(width // LANES):
            cols = slice(j * LANES, (j + 1) * LANES)
            contrast = -(sin_all[:, j : j + 1] * cos_lo + cos_all[:, j : j + 1] * sin_lo)
            scaled = contrast * inv_ref[:, cols]
            for c in range(2):
                image = images_ref[c, rows, cols].astype(jnp.float32)
                weighted_ref[c, rows, cols] = (image * scaled).astype(jnp.bfloat16)
            noise_ref[rows, cols] = (contrast * scaled).astype(jnp.bfloat16)
        for copy in copies_out(i):
            copy.start()
        return 0

    def finish(i, _):
        for copy in copies_out(i):
            copy.wait()
        return 0

    lax.fori_loop(0, steps, start, 0)
    lax.fori_loop(0, steps, body, 0)
    block = proj_ref.shape[0] * proj_ref.shape[3]
    cols = pl.ds(pl.multiple_of(x_ref[0] * block, block), block)
    part_ref[...] = score_terms(
        proj_ref, weighted_ref[0, :, cols], weighted_ref[1, :, cols], noise_ref[:, cols]
    )
    lax.fori_loop(0, steps, finish, 0)


def weight_images(x, images, defocus, inv_sigma2, proj):
    _, n, width = images.shape
    low = jnp.arange(LANES, dtype=jnp.float32) / width
    high = (jnp.arange(LANES, dtype=jnp.float32) * LANES + 0.5) / width
    phase = jnp.concatenate(
        [defocus[:, None] * low[None, :], defocus[:, None] * high[None, :] + 0.1], axis=1
    )
    assert width <= LANES * LANES
    in_hbm, in_vmem = pl.BlockSpec(memory_space=pl.ANY), pl.BlockSpec(memory_space=pltpu.VMEM)
    return pl.pallas_call(
        weight_kernel,
        in_specs=[pl.BlockSpec(memory_space=pltpu.SMEM), in_hbm] + [in_vmem] * 4,
        out_specs=[in_hbm, in_hbm, in_vmem],
        out_shape=[
            jax.ShapeDtypeStruct((2, n, width), jnp.bfloat16),
            jax.ShapeDtypeStruct((n, width), jnp.bfloat16),
            jax.ShapeDtypeStruct((proj.shape[2], n), jnp.float32),
        ],
        scratch_shapes=[
            pltpu.VMEM((2, n, width), jnp.bfloat16),
            pltpu.VMEM((2, n, width), jnp.bfloat16),
            pltpu.VMEM((n, width), jnp.bfloat16),
            pltpu.SemaphoreType.DMA((3, n // WEIGHT_ROWS)),
        ],
        cost_estimate=SMALL_COST,
        compiler_params=pltpu.CompilerParams(vmem_limit_bytes=WEIGHT_VMEM),
        interpret=INTERPRET,
        name="weight_images",
    )(x[None], images, jnp.sin(phase), jnp.cos(phase), inv_sigma2[None, :], proj)


def score_kernel(
    x_ref, proj_hbm, weighted_hbm, noise_hbm, part_ref, bias_ref, scores_ref, log_sum_ref,
    proj_ref, weighted_ref, noise_ref, sems,
):
    n_s, n_z, _, _, slab = proj_ref.shape
    block = n_z * slab

    def copies(i):
        source = (x_ref[0] + i + 1) & (NX - 1)
        cols = pl.ds(pl.multiple_of(source * block, block), block)
        return (
            pltpu.make_async_copy(proj_hbm.at[source], proj_ref.at[i], sems.at[0, i]),
            pltpu.make_async_copy(weighted_hbm.at[:, :, cols], weighted_ref.at[i], sems.at[1, i]),
            pltpu.make_async_copy(noise_hbm.at[:, cols], noise_ref.at[i], sems.at[2, i]),
        )

    for i in range(n_s):
        for copy in copies(i):
            copy.start()
    total = part_ref[...]
    for i in range(n_s):
        for copy in copies(i):
            copy.wait()
        total += score_terms(proj_ref.at[i], weighted_ref[i, 0], weighted_ref[i, 1], noise_ref[i])
    bias = bias_ref[...]
    scores = jnp.where(bias == NEG_FILL, bias, total + bias)
    scores_ref[...] = scores
    peak = jnp.max(scores, axis=0, keepdims=True)
    log_sum = peak + jnp.log(jnp.sum(jnp.exp(scores - peak), axis=0, keepdims=True))
    log_sum_ref[...] = jnp.broadcast_to(log_sum[None], log_sum_ref.shape)


def score(x, proj, weighted, noise, part, bias, copies):
    n_x, n_z, _, rows, slab = proj.shape
    n = weighted.shape[1]
    in_hbm, in_vmem = pl.BlockSpec(memory_space=pl.ANY), pl.BlockSpec(memory_space=pltpu.VMEM)
    return pl.pallas_call(
        score_kernel,
        in_specs=[pl.BlockSpec(memory_space=pltpu.SMEM)] + [in_hbm] * 3 + [in_vmem] * 2,
        out_specs=[in_vmem] * 2,
        out_shape=[
            jax.ShapeDtypeStruct((rows, n), jnp.float32),
            jax.ShapeDtypeStruct((copies, 1, n), jnp.float32),
        ],
        scratch_shapes=[
            pltpu.VMEM((n_x - 1,) + proj.shape[1:], jnp.bfloat16),
            pltpu.VMEM((n_x - 1, 2, n, n_z * slab), jnp.bfloat16),
            pltpu.VMEM((n_x - 1, n, n_z * slab), jnp.bfloat16),
            pltpu.SemaphoreType.DMA((3, n_x - 1)),
        ],
        cost_estimate=SMALL_COST,
        compiler_params=pltpu.CompilerParams(vmem_limit_bytes=MOST_VMEM),
        interpret=INTERPRET,
        name="score",
    )(x[None], proj, weighted, noise, part, bias)


def posterior_kernel(core_ref, scores_hbm, log_sums_ref, post_ref, post_bf_ref, scores_ref, sem):
    copy = pltpu.make_async_copy(scores_hbm, scores_ref, sem)
    copy.start()
    parts = log_sums_ref[...]
    peak = jnp.max(parts, axis=0)
    log_sum = peak + jnp.log(jnp.sum(jnp.exp(parts - peak[None]), axis=0))
    copy.wait()
    posteriors = jnp.exp(scores_ref[...] - log_sum)
    half = posteriors.shape[1] // NC
    swapped = jnp.concatenate([posteriors[:, half:], posteriors[:, :half]], axis=1)
    own_first = jnp.where(core_ref[0] == 0, posteriors, swapped).astype(jnp.bfloat16)
    post_bf_ref[...] = own_first
    post_ref[...] = posteriors.T


def posterior(core, scores, log_sums):
    rows, n = scores.shape
    return pl.pallas_call(
        posterior_kernel,
        in_specs=[
            pl.BlockSpec(memory_space=pltpu.SMEM),
            pl.BlockSpec(memory_space=pl.ANY),
            pl.BlockSpec(memory_space=pltpu.VMEM),
        ],
        out_shape=[
            jax.ShapeDtypeStruct((n, rows), jnp.float32),
            jax.ShapeDtypeStruct((rows, n), jnp.bfloat16),
        ],
        scratch_shapes=[pltpu.VMEM(scores.shape, jnp.float32), pltpu.SemaphoreType.DMA],
        cost_estimate=SMALL_COST,
        compiler_params=pltpu.CompilerParams(vmem_limit_bytes=MOST_VMEM),
        interpret=INTERPRET,
        name="posterior",
    )(core[None], scores, log_sums)


def squared_contrast(defocus, freq2):
    turns = freq2 * (defocus * (1.0 / math.pi)) + 0.1 / math.pi
    return 0.5 - sin_quarter(0.25 - jnp.abs(turns - jnp.round(turns)), 0.5)


def defocus_terms(defocus):
    scaled = defocus * (1.0 / 256.0)
    first = lax.reduce_precision(scaled, 8, 7)
    second = lax.reduce_precision(scaled - first, 8, 7)
    third = scaled - first - second
    return jnp.stack([first, second, third]).astype(jnp.bfloat16)


def squares_of(stacks, freq2):
    parts = []
    half = freq2.shape[1]
    for stack in stacks:
        terms = stack.astype(jnp.float32)
        defocus = (terms[0:1, :half] + terms[1:2, :half] + terms[2:3, :half]) * 256.0
        parts.append(squared_contrast(defocus, freq2).astype(jnp.bfloat16))
    return jnp.concatenate(parts, axis=1)


def back_kernel(sources, ahead, width, start_ref, *refs):
    n_s, last = len(sources), not ahead
    posts, hbm = refs[:n_s], refs[n_s : n_s + 2]
    if last:
        before_ref, squares_ref, out_ref, own_ref, other_ref, sems = refs[n_s + 2 :]
    else:
        out_ref, squares_ref, own_ref, other_ref, terms_ref, sems = refs[n_s + 2 :]
    n_z, _, n = posts[0].shape
    slab, half = out_ref.shape[2], n // NC

    def copies(i):
        return [
            pltpu.make_async_copy(src.at[sources[i]], dst.at[i], sems.at[i, j])
            for j, (src, dst) in enumerate(zip(hbm, (own_ref, other_ref)))
        ]

    def term_copies(i):
        return [
            pltpu.make_async_copy(
                src.at[ahead[i], :, pl.ds(n, TERM_ROWS), :], terms_ref.at[i, j], sems.at[n_s + i, j]
            )
            for j, src in enumerate(hbm)
        ]

    for i in range(n_s):
        for copy in copies(i):
            copy.start()
    for i in range(len(ahead)):
        for copy in term_copies(i):
            copy.start()
    if not last:
        pixel = start_ref[0] + lax.broadcasted_iota(jnp.int32, (slab, half), 0)
        freq2 = (pixel.astype(jnp.float32) + 0.5) * (1.0 / width)
    for i in range(n_s):
        for copy in copies(i):
            copy.wait()
        stacks = [stack[i, t] for t in range(n_z) for stack in (own_ref, other_ref)]
        post = jnp.concatenate([posts[i][t] for t in range(n_z)], axis=1)
        if last:
            square = squares_ref[i]
        else:
            square = squares_of([stack[n : n + TERM_ROWS] for stack in stacks], freq2)
        for c in range(3):
            if c < 2:
                images = [stack[c * half : (c + 1) * half] for stack in stacks]
                total = jnp.dot(
                    post, jnp.concatenate(images, axis=0), preferred_element_type=jnp.float32
                )
            else:
                total = dot_nt(post, square)
            if i > 0:
                total += out_ref[c]
            elif last:
                total += before_ref[c]
            out_ref[c] = total
    for i in range(len(ahead)):
        for copy in term_copies(i):
            copy.wait()
        stacks = [terms_ref[i, j, t] for t in range(n_z) for j in range(2)]
        squares_ref[i] = squares_of(stacks, freq2)


def back_project(start, width, sources, posts, stacks, ahead=(), before=()):
    n_s, (n_z, rows, n) = len(sources), posts[0].shape
    slab = stacks[0].shape[3]
    in_hbm, in_vmem = pl.BlockSpec(memory_space=pl.ANY), pl.BlockSpec(memory_space=pltpu.VMEM)
    out_shape = [jax.ShapeDtypeStruct((3, rows, slab), jnp.float32)]
    scratch = [pltpu.VMEM((n_s,) + stack.shape[1:], jnp.bfloat16) for stack in stacks]
    if ahead:
        n_a = len(ahead)
        out_shape.append(jax.ShapeDtypeStruct((n_a, slab, n_z * n), jnp.bfloat16))
        scratch.append(pltpu.VMEM((n_a, NC, n_z, TERM_ROWS, slab), jnp.bfloat16))
    return pl.pallas_call(
        functools.partial(back_kernel, sources, ahead, width),
        in_specs=[pl.BlockSpec(memory_space=pltpu.SMEM)]
        + [in_vmem] * n_s
        + [in_hbm] * 2
        + [in_vmem] * len(before),
        out_specs=[in_vmem] * len(out_shape),
        out_shape=out_shape,
        scratch_shapes=scratch + [pltpu.SemaphoreType.DMA((n_s + len(ahead), 2))],
        cost_estimate=SMALL_COST,
        compiler_params=pltpu.CompilerParams(vmem_limit_bytes=BACK_VMEM),
        interpret=INTERPRET,
        name="back_project",
    )(start[None], *posts, *stacks, *before)


def exchange(copies, axis, groups=None):
    return lax.all_to_all(copies, axis, 0, 0, axis_index_groups=groups)


def copies_of(value, size):
    return jnp.broadcast_to(value[None], (size,) + value.shape)


def on_device(
    images, projections, defocus, inv_sigma2, log_prior, row_class, pose_block, significant
):
    _, n, width = images.shape
    _, rows, slab = projections.shape
    half = n // NC
    group, pose = lax.axis_index("grp"), lax.axis_index("pose")
    x, zh = group >> 2, group & 3
    y, zl, core = pose >> 3, (pose >> 1) & 3, pose & 1

    z_groups = [[a * NZH + b for b in range(NZH)] for a in range(NX)]
    x_groups = [[a * NZH + b for a in range(NX)] for b in range(NZH)]
    y_groups = [
        [(a * NZL + b) * NC + c for a in range(NY)] for b in range(NZL) for c in range(NC)
    ]
    with jax.named_scope("gather_projections"):
        proj_z = lax.all_gather(projections, "grp", axis=0, axis_index_groups=z_groups)
        proj_z, defocus = lax.optimization_barrier((proj_z, defocus))
        proj = lax.all_gather(proj_z, "grp", axis=0, axis_index_groups=x_groups)

    with jax.named_scope("exchange_images"):
        target = (((x + y) & 3) << 2) + ((zh + zl) & 3)
        cut = lax.dynamic_slice(images, (0, core * half, target * slab), (2, half, slab))
        part_defocus = lax.dynamic_slice(defocus, (core * half,), (half,))
        pixel = (target * slab + jnp.arange(slab)).astype(jnp.float32)
        contrast = -jnp.sin(part_defocus[:, None] * ((pixel + 0.5) / width)[None, :] + 0.1)
        cut = (cut.astype(jnp.float32) * contrast[None]).astype(jnp.bfloat16)
        terms = jnp.pad(defocus_terms(part_defocus), ((0, TERM_ROWS - 3), (0, slab - half)))
        share = jnp.concatenate([cut.reshape(2 * half, slab), terms], axis=0)
        share = lax.ppermute(share, ("grp", "pose"), share_pairs())

    with jax.named_scope("weights"):
        weighted, noise, part = weight_images(x, images, defocus, inv_sigma2, proj_z)
        class_match = row_class[:, None] == jnp.arange(log_prior.shape[0])[None, :]
        prior_rows = jnp.sum(jnp.where(class_match, log_prior[None, :], 0.0), axis=1)
        block_table = pose_block[:, None] == jnp.arange(significant.shape[1])[None, :]
        hits = jnp.einsum(
            "rb,ib->ri",
            block_table.astype(jnp.bfloat16),
            significant.astype(jnp.bfloat16),
            preferred_element_type=jnp.float32,
        )
        bias = jnp.where(hits > 0.5, prior_rows[:, None], jnp.float32(NEG_FILL))

    with jax.named_scope("gather_images"):
        share, part, bias = lax.optimization_barrier((share, part, bias))
        turned = copies_of(share, NZL)
        for d in (1, 2, 3):
            block = lax.ppermute(share, "pose", pose_shift(0, d, 0))
            turned = lax.dynamic_update_slice_in_dim(turned, block[None], (zh - zl + d) & 3, 0)
        turned, proj = lax.optimization_barrier((turned, proj))
        own = lax.all_gather(turned, "pose", axis=0, axis_index_groups=y_groups)

    with jax.named_scope("scores"):
        scores, log_sum = score(x, proj, weighted, noise, part, bias, NY * NZL * NC)

    with jax.named_scope("softmax"):
        posteriors, post_bf = posterior(core, scores, exchange(log_sum, "pose"))

    with jax.named_scope("gather_posteriors"):
        post = [lax.all_gather(post_bf, "grp", axis=0, axis_index_groups=z_groups)] + [None] * 3
        for d in (1, 3, 2):
            post[d] = lax.ppermute(post[0], "grp", grp_shift(d))
        post[0], own = lax.optimization_barrier((post[0], own))
        other = lax.ppermute(own, "pose", pose_shift(0, 0, 1))

    with jax.named_scope("back_project"):
        start, stacks = group * slab, (own, other)
        near, far = (0, 1), (3, 2)
        before = back_project(start, width, near, [post[d] for d in near], stacks, ahead=far)
        (back_proj,) = back_project(start, width, far, [post[d] for d in far], stacks, before=before)
    return (posteriors, back_proj)


def solution(mesh):
    placed = (
        P(None, "grp", None),
        P(None, "pose", "grp"),
        P("grp"),
        P(),
        P(),
        P("pose"),
        P("pose"),
        P("grp", None),
    )
    return jax.shard_map(
        on_device,
        mesh=mesh,
        in_specs=placed,
        out_specs=(P("grp", "pose"), P(None, "pose", "grp")),
        check_vma=False,
    )
```

```python
import functools
import math

import jax
import jax.numpy as jnp
from jax import lax
from jax.experimental import pallas as pl
from jax.experimental.pallas import tpu as pltpu
from jax.sharding import PartitionSpec as P

NEG_FILL = -1e30
NX, NZH = 4, 4
NY, NZL, NC = 4, 4, 2
LANES = 128
TERM_ROWS = 16
MOST_VMEM = 63 << 20
BACK_VMEM = 20 << 20
WEIGHT_VMEM = 60 << 20
SMALL_COST = pl.CostEstimate(flops=1, bytes_accessed=1, transcendentals=0)
INTERPRET = False


def grp_shift(dx):
    return [(x * NZH + z, ((x + dx) % NX) * NZH + z) for x in range(NX) for z in range(NZH)]


def pose_shift(dy, dz, dc):
    return [
        (
            (y * NZL + z) * NC + c,
            (((y + dy) % NY) * NZL + (z + dz) % NZL) * NC + (c + dc) % NC,
        )
        for y in range(NY)
        for z in range(NZL)
        for c in range(NC)
    ]


def share_pairs():
    n_pose = NY * NZL * NC
    pairs = []
    for x in range(NX):
        for zh in range(NZH):
            for y in range(NY):
                for zl in range(NZL):
                    for c in range(NC):
                        pose = (y * NZL + zl) * NC + c
                        src = x * NZH + zh
                        dst = ((x + y) % NX) * NZH + (zh + zl) % NZH
                        pairs.append((src * n_pose + pose, dst * n_pose + pose))
    return pairs


SIN_TERMS = tuple(
    (-1) ** n * (2 * math.pi) ** (2 * n + 1) / math.factorial(2 * n + 1) for n in range(7)
)


def sin_quarter(t, scale=1.0):
    square = t * t
    value = square * (scale * SIN_TERMS[-1]) + scale * SIN_TERMS[-2]
    for term in SIN_TERMS[-3::-1]:
        value = value * square + scale * term
    return value * t


WEIGHT_ROWS = 32


def dot_nt(a, b):
    return lax.dot_general(a, b, (((1,), (1,)), ((), ())), preferred_element_type=jnp.float32)


def score_terms(proj, weighted_real, weighted_imag, noise):
    n_z = proj.shape[0]
    real = jnp.concatenate([proj[z, 0] for z in range(n_z)], axis=1)
    imag = jnp.concatenate([proj[z, 1] for z in range(n_z)], axis=1)
    real_f, imag_f = real.astype(jnp.float32), imag.astype(jnp.float32)
    power = (real_f * real_f + imag_f * imag_f).astype(jnp.bfloat16)
    return dot_nt(real, weighted_real) + dot_nt(imag, weighted_imag) - 0.5 * dot_nt(power, noise)


def weight_kernel(
    x_ref, images_hbm, sin_ref, cos_ref, inv_ref, proj_ref, weighted_hbm, noise_hbm, part_ref,
    images_ref, weighted_ref, noise_ref, sems,
):
    n, width = images_ref.shape[1:]
    steps = n // WEIGHT_ROWS

    def rows_of(i):
        return pl.ds(pl.multiple_of(i * WEIGHT_ROWS, WEIGHT_ROWS), WEIGHT_ROWS)

    def copy_in(i):
        rows = rows_of(i)
        return pltpu.make_async_copy(
            images_hbm.at[:, rows, :], images_ref.at[:, rows, :], sems.at[0, i]
        )

    def copies_out(i):
        rows = rows_of(i)
        return (
            pltpu.make_async_copy(
                weighted_ref.at[:, rows, :], weighted_hbm.at[:, rows, :], sems.at[1, i]
            ),
            pltpu.make_async_copy(noise_ref.at[rows, :], noise_hbm.at[rows, :], sems.at[2, i]),
        )

    def start(i, _):
        copy_in(i).start()
        return 0

    def body(i, _):
        copy_in(i).wait()
        rows = rows_of(i)
        sin_lo, cos_lo = sin_ref[rows, :LANES], cos_ref[rows, :LANES]
        sin_all, cos_all = sin_ref[rows, LANES:], cos_ref[rows, LANES:]
        for j in range(width // LANES):
            cols = slice(j * LANES, (j + 1) * LANES)
            contrast = -(sin_all[:, j : j + 1] * cos_lo + cos_all[:, j : j + 1] * sin_lo)
            scaled = contrast * inv_ref[:, cols]
            for c in range(2):
                image = images_ref[c, rows, cols].astype(jnp.float32)
                weighted_ref[c, rows, cols] = (image * scaled).astype(jnp.bfloat16)
            noise_ref[rows, cols] = (contrast * scaled).astype(jnp.bfloat16)
        for copy in copies_out(i):
            copy.start()
        return 0

    def finish(i, _):
        for copy in copies_out(i):
            copy.wait()
        return 0

    lax.fori_loop(0, steps, start, 0)
    lax.fori_loop(0, steps, body, 0)
    block = proj_ref.shape[0] * proj_ref.shape[3]
    cols = pl.ds(pl.multiple_of(x_ref[0] * block, block), block)
    part_ref[...] = score_terms(
        proj_ref, weighted_ref[0, :, cols], weighted_ref[1, :, cols], noise_ref[:, cols]
    )
    lax.fori_loop(0, steps, finish, 0)


def weight_images(x, images, defocus, inv_sigma2, proj):
    _, n, width = images.shape
    low = jnp.arange(LANES, dtype=jnp.float32) / width
    high = (jnp.arange(LANES, dtype=jnp.float32) * LANES + 0.5) / width
    phase = jnp.concatenate(
        [defocus[:, None] * low[None, :], defocus[:, None] * high[None, :] + 0.1], axis=1
    )
    assert width <= LANES * LANES
    in_hbm, in_vmem = pl.BlockSpec(memory_space=pl.ANY), pl.BlockSpec(memory_space=pltpu.VMEM)
    return pl.pallas_call(
        weight_kernel,
        in_specs=[pl.BlockSpec(memory_space=pltpu.SMEM), in_hbm] + [in_vmem] * 4,
        out_specs=[in_hbm, in_hbm, in_vmem],
        out_shape=[
            jax.ShapeDtypeStruct((2, n, width), jnp.bfloat16),
            jax.ShapeDtypeStruct((n, width), jnp.bfloat16),
            jax.ShapeDtypeStruct((proj.shape[2], n), jnp.float32),
        ],
        scratch_shapes=[
            pltpu.VMEM((2, n, width), jnp.bfloat16),
            pltpu.VMEM((2, n, width), jnp.bfloat16),
            pltpu.VMEM((n, width), jnp.bfloat16),
            pltpu.SemaphoreType.DMA((3, n // WEIGHT_ROWS)),
        ],
        cost_estimate=SMALL_COST,
        compiler_params=pltpu.CompilerParams(vmem_limit_bytes=WEIGHT_VMEM),
        interpret=INTERPRET,
        name="weight_images",
    )(x[None], images, jnp.sin(phase), jnp.cos(phase), inv_sigma2[None, :], proj)


def score_kernel(
    x_ref, proj_hbm, weighted_hbm, noise_hbm, part_ref, bias_ref, scores_ref, log_sum_ref,
    proj_ref, weighted_ref, noise_ref, sems,
):
    n_s, n_z, _, _, slab = proj_ref.shape
    block = n_z * slab

    def copies(i):
        source = (x_ref[0] + i + 1) & (NX - 1)
        cols = pl.ds(pl.multiple_of(source * block, block), block)
        return (
            pltpu.make_async_copy(proj_hbm.at[source], proj_ref.at[i], sems.at[0, i]),
            pltpu.make_async_copy(weighted_hbm.at[:, :, cols], weighted_ref.at[i], sems.at[1, i]),
            pltpu.make_async_copy(noise_hbm.at[:, cols], noise_ref.at[i], sems.at[2, i]),
        )

    for i in range(n_s):
        for copy in copies(i):
            copy.start()
    total = part_ref[...]
    for i in range(n_s):
        for copy in copies(i):
            copy.wait()
        total += score_terms(proj_ref.at[i], weighted_ref[i, 0], weighted_ref[i, 1], noise_ref[i])
    bias = bias_ref[...]
    scores = jnp.where(bias == NEG_FILL, bias, total + bias)
    scores_ref[...] = scores
    peak = jnp.max(scores, axis=0, keepdims=True)
    log_sum = peak + jnp.log(jnp.sum(jnp.exp(scores - peak), axis=0, keepdims=True))
    log_sum_ref[...] = jnp.broadcast_to(log_sum[None], log_sum_ref.shape)


def score(x, proj, weighted, noise, part, bias, copies):
    n_x, n_z, _, rows, slab = proj.shape
    n = weighted.shape[1]
    in_hbm, in_vmem = pl.BlockSpec(memory_space=pl.ANY), pl.BlockSpec(memory_space=pltpu.VMEM)
    return pl.pallas_call(
        score_kernel,
        in_specs=[pl.BlockSpec(memory_space=pltpu.SMEM)] + [in_hbm] * 3 + [in_vmem] * 2,
        out_specs=[in_vmem] * 2,
        out_shape=[
            jax.ShapeDtypeStruct((rows, n), jnp.float32),
            jax.ShapeDtypeStruct((copies, 1, n), jnp.float32),
        ],
        scratch_shapes=[
            pltpu.VMEM((n_x - 1,) + proj.shape[1:], jnp.bfloat16),
            pltpu.VMEM((n_x - 1, 2, n, n_z * slab), jnp.bfloat16),
            pltpu.VMEM((n_x - 1, n, n_z * slab), jnp.bfloat16),
            pltpu.SemaphoreType.DMA((3, n_x - 1)),
        ],
        cost_estimate=SMALL_COST,
        compiler_params=pltpu.CompilerParams(vmem_limit_bytes=MOST_VMEM),
        interpret=INTERPRET,
        name="score",
    )(x[None], proj, weighted, noise, part, bias)


def posterior_kernel(core_ref, scores_hbm, log_sums_ref, post_ref, post_bf_ref, scores_ref, sem):
    copy = pltpu.make_async_copy(scores_hbm, scores_ref, sem)
    copy.start()
    parts = log_sums_ref[...]
    peak = jnp.max(parts, axis=0)
    log_sum = peak + jnp.log(jnp.sum(jnp.exp(parts - peak[None]), axis=0))
    copy.wait()
    posteriors = jnp.exp(scores_ref[...] - log_sum)
    half = posteriors.shape[1] // NC
    swapped = jnp.concatenate([posteriors[:, half:], posteriors[:, :half]], axis=1)
    own_first = jnp.where(core_ref[0] == 0, posteriors, swapped).astype(jnp.bfloat16)
    post_bf_ref[...] = own_first
    post_ref[...] = posteriors.T


def posterior(core, scores, log_sums):
    rows, n = scores.shape
    return pl.pallas_call(
        posterior_kernel,
        in_specs=[
            pl.BlockSpec(memory_space=pltpu.SMEM),
            pl.BlockSpec(memory_space=pl.ANY),
            pl.BlockSpec(memory_space=pltpu.VMEM),
        ],
        out_shape=[
            jax.ShapeDtypeStruct((n, rows), jnp.float32),
            jax.ShapeDtypeStruct((rows, n), jnp.bfloat16),
        ],
        scratch_shapes=[pltpu.VMEM(scores.shape, jnp.float32), pltpu.SemaphoreType.DMA],
        cost_estimate=SMALL_COST,
        compiler_params=pltpu.CompilerParams(vmem_limit_bytes=MOST_VMEM),
        interpret=INTERPRET,
        name="posterior",
    )(core[None], scores, log_sums)


def squared_contrast(defocus, freq2):
    turns = freq2 * (defocus * (1.0 / math.pi)) + 0.1 / math.pi
    return 0.5 - sin_quarter(0.25 - jnp.abs(turns - jnp.round(turns)), 0.5)


def defocus_terms(defocus):
    scaled = defocus * (1.0 / 256.0)
    first = lax.reduce_precision(scaled, 8, 7)
    second = lax.reduce_precision(scaled - first, 8, 7)
    third = scaled - first - second
    return jnp.stack([first, second, third]).astype(jnp.bfloat16)


def squares_of(stacks, freq2):
    parts = []
    half = freq2.shape[1]
    for stack in stacks:
        terms = stack.astype(jnp.float32)
        defocus = (terms[0:1, :half] + terms[1:2, :half] + terms[2:3, :half]) * 256.0
        parts.append(squared_contrast(defocus, freq2).astype(jnp.bfloat16))
    return jnp.concatenate(parts, axis=1)


def back_kernel(sources, ahead, width, start_ref, *refs):
    last = not ahead
    n_s = len(sources)
    posts, images = refs[:n_s], refs[n_s : n_s + 2]
    if last:
        before_ref, squares_ref, out_ref = refs[n_s + 2 :]
    else:
        out_ref, squares_ref = refs[n_s + 2 :]
    n_z, _, n = posts[0].shape
    slab, half = out_ref.shape[2], n // NC

    def stacked(source, first, size):
        rows = slice(first, first + size)
        return [ref[source, t, rows] for t in range(n_z) for ref in images]

    if not last:
        pixel = start_ref[0] + lax.broadcasted_iota(jnp.int32, (slab, half), 0)
        freq2 = (pixel.astype(jnp.float32) + 0.5) * (1.0 / width)
    for i, source in enumerate(sources):
        post = jnp.concatenate([posts[i][t] for t in range(n_z)], axis=1)
        for c in range(3):
            if c < 2:
                image = jnp.concatenate(stacked(source, c * half, half), axis=0)
                total = jnp.dot(post, image, preferred_element_type=jnp.float32)
            elif last:
                total = dot_nt(post, squares_ref[i])
            else:
                total = dot_nt(post, squares_of(stacked(source, n, TERM_ROWS), freq2))
            if i > 0:
                total += out_ref[c]
            elif last:
                total += before_ref[c]
            out_ref[c] = total
    for i, source in enumerate(ahead):
        squares_ref[i] = squares_of(stacked(source, n, TERM_ROWS), freq2)


def back_project(start, width, sources, posts, images, ahead=(), before=()):
    n_z, rows, n = posts[0].shape
    slab = images[0].shape[3]
    in_vmem = pl.BlockSpec(memory_space=pltpu.VMEM)
    out_shape = [jax.ShapeDtypeStruct((3, rows, slab), jnp.float32)]
    if ahead:
        out_shape.append(jax.ShapeDtypeStruct((len(ahead), slab, n_z * n), jnp.bfloat16))
    return pl.pallas_call(
        functools.partial(back_kernel, sources, ahead, width),
        in_specs=[pl.BlockSpec(memory_space=pltpu.SMEM)]
        + [in_vmem] * (len(sources) + 2 + len(before)),
        out_specs=[in_vmem] * len(out_shape),
        out_shape=out_shape,
        cost_estimate=SMALL_COST,
        compiler_params=pltpu.CompilerParams(vmem_limit_bytes=BACK_VMEM),
        interpret=INTERPRET,
        name="back_project",
    )(start[None], *posts, *images, *before)


def exchange(copies, axis, groups=None):
    return lax.all_to_all(copies, axis, 0, 0, axis_index_groups=groups)


def copies_of(value, size):
    return jnp.broadcast_to(value[None], (size,) + value.shape)


def on_device(
    images, projections, defocus, inv_sigma2, log_prior, row_class, pose_block, significant
):
    _, n, width = images.shape
    _, rows, slab = projections.shape
    half = n // NC
    group, pose = lax.axis_index("grp"), lax.axis_index("pose")
    x, zh = group >> 2, group & 3
    y, zl, core = pose >> 3, (pose >> 1) & 3, pose & 1

    z_groups = [[a * NZH + b for b in range(NZH)] for a in range(NX)]
    x_groups = [[a * NZH + b for a in range(NX)] for b in range(NZH)]
    y_groups = [
        [(a * NZL + b) * NC + c for a in range(NY)] for b in range(NZL) for c in range(NC)
    ]
    with jax.named_scope("gather_projections"):
        proj_z = lax.all_gather(projections, "grp", axis=0, axis_index_groups=z_groups)
        proj_z, defocus = lax.optimization_barrier((proj_z, defocus))
        proj = lax.all_gather(proj_z, "grp", axis=0, axis_index_groups=x_groups)

    with jax.named_scope("exchange_images"):
        target = (((x + y) & 3) << 2) + ((zh + zl) & 3)
        cut = lax.dynamic_slice(images, (0, core * half, target * slab), (2, half, slab))
        part_defocus = lax.dynamic_slice(defocus, (core * half,), (half,))
        pixel = (target * slab + jnp.arange(slab)).astype(jnp.float32)
        contrast = -jnp.sin(part_defocus[:, None] * ((pixel + 0.5) / width)[None, :] + 0.1)
        cut = (cut.astype(jnp.float32) * contrast[None]).astype(jnp.bfloat16)
        terms = jnp.pad(defocus_terms(part_defocus), ((0, TERM_ROWS - 3), (0, slab - half)))
        share = jnp.concatenate([cut.reshape(2 * half, slab), terms], axis=0)
        share = lax.ppermute(share, ("grp", "pose"), share_pairs())

    with jax.named_scope("weights"):
        weighted, noise, part = weight_images(x, images, defocus, inv_sigma2, proj_z)
        class_match = row_class[:, None] == jnp.arange(log_prior.shape[0])[None, :]
        prior_rows = jnp.sum(jnp.where(class_match, log_prior[None, :], 0.0), axis=1)
        block_table = pose_block[:, None] == jnp.arange(significant.shape[1])[None, :]
        hits = jnp.einsum(
            "rb,ib->ri",
            block_table.astype(jnp.bfloat16),
            significant.astype(jnp.bfloat16),
            preferred_element_type=jnp.float32,
        )
        bias = jnp.where(hits > 0.5, prior_rows[:, None], jnp.float32(NEG_FILL))

    with jax.named_scope("gather_images"):
        share, part, bias = lax.optimization_barrier((share, part, bias))
        turned = copies_of(share, NZL)
        for d in (1, 2, 3):
            block = lax.ppermute(share, "pose", pose_shift(0, d, 0))
            turned = lax.dynamic_update_slice_in_dim(turned, block[None], (zh - zl + d) & 3, 0)
        turned, proj = lax.optimization_barrier((turned, proj))
        own = lax.all_gather(turned, "pose", axis=0, axis_index_groups=y_groups)

    with jax.named_scope("scores"):
        scores, log_sum = score(x, proj, weighted, noise, part, bias, NY * NZL * NC)

    with jax.named_scope("softmax"):
        posteriors, post_bf = posterior(core, scores, exchange(log_sum, "pose"))

    with jax.named_scope("gather_posteriors"):
        post = [lax.all_gather(post_bf, "grp", axis=0, axis_index_groups=z_groups)] + [None] * 3
        for d in (1, 3, 2):
            post[d] = lax.ppermute(post[0], "grp", grp_shift(d))
        post[0], own = lax.optimization_barrier((post[0], own))
        other = lax.ppermute(own, "pose", pose_shift(0, 0, 1))

    with jax.named_scope("back_project"):
        start = group * slab
        near, far, stacks = (0,), (1, 3, 2), (own, other)
        before = back_project(start, width, near, [post[d] for d in near], stacks, ahead=far)
        (back_proj,) = back_project(start, width, far, [post[d] for d in far], stacks, before=before)
    return (posteriors, back_proj)


def solution(mesh):
    placed = (
        P(None, "grp", None),
        P(None, "pose", "grp"),
        P("grp"),
        P(),
        P(),
        P("pose"),
        P("pose"),
        P("grp", None),
    )
    return jax.shard_map(
        on_device,
        mesh=mesh,
        in_specs=placed,
        out_specs=(P("grp", "pose"), P(None, "pose", "grp")),
        check_vma=False,
    )
```

```python
import functools
import math

import jax
import jax.numpy as jnp
from jax import lax
from jax.experimental import pallas as pl
from jax.experimental.pallas import tpu as pltpu
from jax.sharding import PartitionSpec as P

NEG_FILL = -1e30
NX, NZH = 4, 4
NY, NZL, NC = 4, 4, 2
LANES = 128
TERM_ROWS = 16
MOST_VMEM = 63 << 20
SMALL_VMEM = 20 << 20
WEIGHT_VMEM = 60 << 20
SMALL_COST = pl.CostEstimate(flops=1, bytes_accessed=1, transcendentals=0)
INTERPRET = False


def grp_shift(dx):
    return [(x * NZH + z, ((x + dx) % NX) * NZH + z) for x in range(NX) for z in range(NZH)]


def pose_shift(dy, dz, dc):
    return [
        (
            (y * NZL + z) * NC + c,
            (((y + dy) % NY) * NZL + (z + dz) % NZL) * NC + (c + dc) % NC,
        )
        for y in range(NY)
        for z in range(NZL)
        for c in range(NC)
    ]


def share_pairs():
    n_pose = NY * NZL * NC
    pairs = []
    for x in range(NX):
        for zh in range(NZH):
            for y in range(NY):
                for zl in range(NZL):
                    for c in range(NC):
                        src = (x * NZH + zh) * n_pose + (y * NZL + zl) * NC + c
                        dst = (((x + y) % NX) * NZH + zl) * n_pose + (y * NZL + zh) * NC + c
                        pairs.append((src, dst))
    return pairs


SIN_TERMS = tuple(
    (-1) ** n * (2 * math.pi) ** (2 * n + 1) / math.factorial(2 * n + 1) for n in range(7)
)


def sin_quarter(t, scale=1.0):
    square = t * t
    value = square * (scale * SIN_TERMS[-1]) + scale * SIN_TERMS[-2]
    for term in SIN_TERMS[-3::-1]:
        value = value * square + scale * term
    return value * t


WEIGHT_ROWS = 32


def dot_nt(a, b):
    return lax.dot_general(a, b, (((1,), (1,)), ((), ())), preferred_element_type=jnp.float32)


def score_terms(proj, weighted_real, weighted_imag, noise):
    n_z = proj.shape[0]
    real = jnp.concatenate([proj[z, 0] for z in range(n_z)], axis=1)
    imag = jnp.concatenate([proj[z, 1] for z in range(n_z)], axis=1)
    real_f, imag_f = real.astype(jnp.float32), imag.astype(jnp.float32)
    power = (real_f * real_f + imag_f * imag_f).astype(jnp.bfloat16)
    return dot_nt(real, weighted_real) + dot_nt(imag, weighted_imag) - 0.5 * dot_nt(power, noise)


def weight_kernel(
    x_ref, images_hbm, sin_ref, cos_ref, inv_ref, proj_ref, weighted_hbm, noise_hbm, part_ref,
    images_ref, weighted_ref, noise_ref, sems,
):
    n, width = images_ref.shape[1:]
    steps = n // WEIGHT_ROWS

    def rows_of(i):
        return pl.ds(pl.multiple_of(i * WEIGHT_ROWS, WEIGHT_ROWS), WEIGHT_ROWS)

    def copy_in(i):
        rows = rows_of(i)
        return pltpu.make_async_copy(
            images_hbm.at[:, rows, :], images_ref.at[:, rows, :], sems.at[0, i]
        )

    def copies_out(i):
        rows = rows_of(i)
        return (
            pltpu.make_async_copy(
                weighted_ref.at[:, rows, :], weighted_hbm.at[:, rows, :], sems.at[1, i]
            ),
            pltpu.make_async_copy(noise_ref.at[rows, :], noise_hbm.at[rows, :], sems.at[2, i]),
        )

    def start(i, _):
        copy_in(i).start()
        return 0

    def body(i, _):
        copy_in(i).wait()
        rows = rows_of(i)
        sin_lo, cos_lo = sin_ref[rows, :LANES], cos_ref[rows, :LANES]
        sin_all, cos_all = sin_ref[rows, LANES:], cos_ref[rows, LANES:]
        for j in range(width // LANES):
            cols = slice(j * LANES, (j + 1) * LANES)
            contrast = -(sin_all[:, j : j + 1] * cos_lo + cos_all[:, j : j + 1] * sin_lo)
            scaled = contrast * inv_ref[:, cols]
            for c in range(2):
                image = images_ref[c, rows, cols].astype(jnp.float32)
                weighted_ref[c, rows, cols] = (image * scaled).astype(jnp.bfloat16)
            noise_ref[rows, cols] = (contrast * scaled).astype(jnp.bfloat16)
        for copy in copies_out(i):
            copy.start()
        return 0

    def finish(i, _):
        for copy in copies_out(i):
            copy.wait()
        return 0

    lax.fori_loop(0, steps, start, 0)
    lax.fori_loop(0, steps, body, 0)
    block = proj_ref.shape[0] * proj_ref.shape[3]
    cols = pl.ds(pl.multiple_of(x_ref[0] * block, block), block)
    part_ref[...] = score_terms(
        proj_ref, weighted_ref[0, :, cols], weighted_ref[1, :, cols], noise_ref[:, cols]
    )
    lax.fori_loop(0, steps, finish, 0)


def weight_images(x, images, defocus, inv_sigma2, proj):
    _, n, width = images.shape
    low = jnp.arange(LANES, dtype=jnp.float32) / width
    high = (jnp.arange(LANES, dtype=jnp.float32) * LANES + 0.5) / width
    phase = jnp.concatenate(
        [defocus[:, None] * low[None, :], defocus[:, None] * high[None, :] + 0.1], axis=1
    )
    assert width <= LANES * LANES
    in_hbm, in_vmem = pl.BlockSpec(memory_space=pl.ANY), pl.BlockSpec(memory_space=pltpu.VMEM)
    return pl.pallas_call(
        weight_kernel,
        in_specs=[pl.BlockSpec(memory_space=pltpu.SMEM), in_hbm] + [in_vmem] * 4,
        out_specs=[in_hbm, in_hbm, in_vmem],
        out_shape=[
            jax.ShapeDtypeStruct((2, n, width), jnp.bfloat16),
            jax.ShapeDtypeStruct((n, width), jnp.bfloat16),
            jax.ShapeDtypeStruct((proj.shape[2], n), jnp.float32),
        ],
        scratch_shapes=[
            pltpu.VMEM((2, n, width), jnp.bfloat16),
            pltpu.VMEM((2, n, width), jnp.bfloat16),
            pltpu.VMEM((n, width), jnp.bfloat16),
            pltpu.SemaphoreType.DMA((3, n // WEIGHT_ROWS)),
        ],
        cost_estimate=SMALL_COST,
        compiler_params=pltpu.CompilerParams(vmem_limit_bytes=WEIGHT_VMEM),
        interpret=INTERPRET,
        name="weight_images",
    )(x[None], images, jnp.sin(phase), jnp.cos(phase), inv_sigma2[None, :], proj)


def score_kernel(
    x_ref, proj_hbm, weighted_hbm, noise_hbm, part_ref, bias_ref, scores_ref, log_sum_ref,
    proj_ref, weighted_ref, noise_ref, sems,
):
    n_s, n_z, _, _, slab = proj_ref.shape
    block = n_z * slab

    def copies(i):
        source = (x_ref[0] + i + 1) & (NX - 1)
        cols = pl.ds(pl.multiple_of(source * block, block), block)
        return (
            pltpu.make_async_copy(proj_hbm.at[source], proj_ref.at[i], sems.at[0, i]),
            pltpu.make_async_copy(weighted_hbm.at[:, :, cols], weighted_ref.at[i], sems.at[1, i]),
            pltpu.make_async_copy(noise_hbm.at[:, cols], noise_ref.at[i], sems.at[2, i]),
        )

    for i in range(n_s):
        for copy in copies(i):
            copy.start()
    total = part_ref[...]
    for i in range(n_s):
        for copy in copies(i):
            copy.wait()
        total += score_terms(proj_ref.at[i], weighted_ref[i, 0], weighted_ref[i, 1], noise_ref[i])
    bias = bias_ref[...]
    scores = jnp.where(bias == NEG_FILL, bias, total + bias)
    scores_ref[...] = scores
    peak = jnp.max(scores, axis=0, keepdims=True)
    log_sum = peak + jnp.log(jnp.sum(jnp.exp(scores - peak), axis=0, keepdims=True))
    log_sum_ref[...] = jnp.broadcast_to(log_sum[None], log_sum_ref.shape)


def score(x, proj, weighted, noise, part, bias, copies):
    n_x, n_z, _, rows, slab = proj.shape
    n = weighted.shape[1]
    in_hbm, in_vmem = pl.BlockSpec(memory_space=pl.ANY), pl.BlockSpec(memory_space=pltpu.VMEM)
    return pl.pallas_call(
        score_kernel,
        in_specs=[pl.BlockSpec(memory_space=pltpu.SMEM)] + [in_hbm] * 3 + [in_vmem] * 2,
        out_specs=[in_vmem] * 2,
        out_shape=[
            jax.ShapeDtypeStruct((rows, n), jnp.float32),
            jax.ShapeDtypeStruct((copies, 1, n), jnp.float32),
        ],
        scratch_shapes=[
            pltpu.VMEM((n_x - 1,) + proj.shape[1:], jnp.bfloat16),
            pltpu.VMEM((n_x - 1, 2, n, n_z * slab), jnp.bfloat16),
            pltpu.VMEM((n_x - 1, n, n_z * slab), jnp.bfloat16),
            pltpu.SemaphoreType.DMA((3, n_x - 1)),
        ],
        cost_estimate=SMALL_COST,
        compiler_params=pltpu.CompilerParams(vmem_limit_bytes=MOST_VMEM),
        interpret=INTERPRET,
        name="score",
    )(x[None], proj, weighted, noise, part, bias)


def posterior_kernel(core_ref, scores_ref, log_sums_ref, post_ref, post_bf_ref):
    parts = log_sums_ref[...]
    peak = jnp.max(parts, axis=0)
    log_sum = peak + jnp.log(jnp.sum(jnp.exp(parts - peak[None]), axis=0))
    posteriors = jnp.exp(scores_ref[...] - log_sum)
    half = posteriors.shape[1] // NC
    swapped = jnp.concatenate([posteriors[:, half:], posteriors[:, :half]], axis=1)
    own_first = jnp.where(core_ref[0] == 0, posteriors, swapped).astype(jnp.bfloat16)
    post_bf_ref[...] = own_first
    post_ref[...] = posteriors.T


def posterior(core, scores, log_sums):
    rows, n = scores.shape
    return pl.pallas_call(
        posterior_kernel,
        in_specs=[
            pl.BlockSpec(memory_space=pltpu.SMEM),
            pl.BlockSpec(memory_space=pltpu.VMEM),
            pl.BlockSpec(memory_space=pltpu.VMEM),
        ],
        out_shape=[
            jax.ShapeDtypeStruct((n, rows), jnp.float32),
            jax.ShapeDtypeStruct((rows, n), jnp.bfloat16),
        ],
        cost_estimate=SMALL_COST,
        compiler_params=pltpu.CompilerParams(vmem_limit_bytes=SMALL_VMEM),
        interpret=INTERPRET,
        name="posterior",
    )(core[None], scores, log_sums)


def squared_contrast(defocus, freq2):
    turns = freq2 * (defocus * (1.0 / math.pi)) + 0.1 / math.pi
    return 0.5 - sin_quarter(0.25 - jnp.abs(turns - jnp.round(turns)), 0.5)


def defocus_terms(defocus):
    scaled = defocus * (1.0 / 256.0)
    first = lax.reduce_precision(scaled, 8, 7)
    second = lax.reduce_precision(scaled - first, 8, 7)
    third = scaled - first - second
    return jnp.stack([first, second, third]).astype(jnp.bfloat16)


def squares_of(stacks, freq2):
    parts = []
    half = freq2.shape[1]
    for stack in stacks:
        terms = stack.astype(jnp.float32)
        defocus = (terms[0:1, :half] + terms[1:2, :half] + terms[2:3, :half]) * 256.0
        parts.append(squared_contrast(defocus, freq2).astype(jnp.bfloat16))
    return jnp.concatenate(parts, axis=1)


def back_kernel(sources, ahead, width, start_ref, *refs):
    last = not ahead
    n_s = len(sources)
    posts, images = refs[:n_s], refs[n_s : n_s + 2]
    if last:
        before_ref, squares_ref, out_ref = refs[n_s + 2 :]
    else:
        out_ref, squares_ref = refs[n_s + 2 :]
    n_z, _, n = posts[0].shape
    slab, half = out_ref.shape[2], n // NC

    def stacked(source, first, size):
        rows = slice(first, first + size)
        return [ref[source, t, rows] for t in range(n_z) for ref in images]

    if not last:
        pixel = start_ref[0] + lax.broadcasted_iota(jnp.int32, (slab, half), 0)
        freq2 = (pixel.astype(jnp.float32) + 0.5) * (1.0 / width)
    for i, source in enumerate(sources):
        post = jnp.concatenate([posts[i][t] for t in range(n_z)], axis=1)
        for c in range(3):
            if c < 2:
                image = jnp.concatenate(stacked(source, c * half, half), axis=0)
                total = jnp.dot(post, image, preferred_element_type=jnp.float32)
            elif last:
                total = dot_nt(post, squares_ref[i])
            else:
                total = dot_nt(post, squares_of(stacked(source, n, TERM_ROWS), freq2))
            if i > 0:
                total += out_ref[c]
            elif last:
                total += before_ref[c]
            out_ref[c] = total
    for i, source in enumerate(ahead):
        squares_ref[i] = squares_of(stacked(source, n, TERM_ROWS), freq2)


def back_project(start, width, sources, posts, images, ahead=(), before=()):
    n_z, rows, n = posts[0].shape
    slab = images[0].shape[3]
    in_vmem = pl.BlockSpec(memory_space=pltpu.VMEM)
    out_shape = [jax.ShapeDtypeStruct((3, rows, slab), jnp.float32)]
    if ahead:
        out_shape.append(jax.ShapeDtypeStruct((len(ahead), slab, n_z * n), jnp.bfloat16))
    return pl.pallas_call(
        functools.partial(back_kernel, sources, ahead, width),
        in_specs=[pl.BlockSpec(memory_space=pltpu.SMEM)]
        + [in_vmem] * (len(sources) + 2 + len(before)),
        out_specs=[in_vmem] * len(out_shape),
        out_shape=out_shape,
        cost_estimate=SMALL_COST,
        compiler_params=pltpu.CompilerParams(vmem_limit_bytes=SMALL_VMEM),
        interpret=INTERPRET,
        name="back_project",
    )(start[None], *posts, *images, *before)


def exchange(copies, axis, groups=None):
    return lax.all_to_all(copies, axis, 0, 0, axis_index_groups=groups)


def copies_of(value, size):
    return jnp.broadcast_to(value[None], (size,) + value.shape)


def on_device(
    images, projections, defocus, inv_sigma2, log_prior, row_class, pose_block, significant
):
    _, n, width = images.shape
    _, rows, slab = projections.shape
    half = n // NC
    group, pose = lax.axis_index("grp"), lax.axis_index("pose")
    x = group >> 2
    y, zl, core = pose >> 3, (pose >> 1) & 3, pose & 1

    z_groups = [[a * NZH + b for b in range(NZH)] for a in range(NX)]
    x_groups = [[a * NZH + b for a in range(NX)] for b in range(NZH)]
    y_groups = [
        [(a * NZL + b) * NC + c for a in range(NY)] for b in range(NZL) for c in range(NC)
    ]
    with jax.named_scope("gather_projections"):
        proj_z = lax.all_gather(projections, "grp", axis=0, axis_index_groups=z_groups)
        proj_z, defocus = lax.optimization_barrier((proj_z, defocus))
        proj = lax.all_gather(proj_z, "grp", axis=0, axis_index_groups=x_groups)

    with jax.named_scope("exchange_images"):
        target = (((x + y) & 3) << 2) + zl
        cut = lax.dynamic_slice(images, (0, core * half, target * slab), (2, half, slab))
        part_defocus = lax.dynamic_slice(defocus, (core * half,), (half,))
        pixel = (target * slab + jnp.arange(slab)).astype(jnp.float32)
        contrast = -jnp.sin(part_defocus[:, None] * ((pixel + 0.5) / width)[None, :] + 0.1)
        cut = (cut.astype(jnp.float32) * contrast[None]).astype(jnp.bfloat16)
        terms = jnp.pad(defocus_terms(part_defocus), ((0, TERM_ROWS - 3), (0, slab - half)))
        share = jnp.concatenate([cut.reshape(2 * half, slab), terms], axis=0)
        share = lax.ppermute(share, ("grp", "pose"), share_pairs())

    with jax.named_scope("weights"):
        weighted, noise, part = weight_images(x, images, defocus, inv_sigma2, proj_z)
        class_match = row_class[:, None] == jnp.arange(log_prior.shape[0])[None, :]
        prior_rows = jnp.sum(jnp.where(class_match, log_prior[None, :], 0.0), axis=1)
        block_table = pose_block[:, None] == jnp.arange(significant.shape[1])[None, :]
        hits = jnp.einsum(
            "rb,ib->ri",
            block_table.astype(jnp.bfloat16),
            significant.astype(jnp.bfloat16),
            preferred_element_type=jnp.float32,
        )
        bias = jnp.where(hits > 0.5, prior_rows[:, None], jnp.float32(NEG_FILL))

    with jax.named_scope("gather_images"):
        share, part, bias = lax.optimization_barrier((share, part, bias))
        turned = copies_of(share, NZL)
        for d in (1, 2, 3):
            block = lax.ppermute(share, "pose", pose_shift(0, d, 0))
            turned = lax.dynamic_update_slice_in_dim(turned, block[None], (zl - d) & 3, 0)
        turned, proj = lax.optimization_barrier((turned, proj))
        own = lax.all_gather(turned, "pose", axis=0, axis_index_groups=y_groups)

    with jax.named_scope("scores"):
        scores, log_sum = score(x, proj, weighted, noise, part, bias, NY * NZL * NC)

    with jax.named_scope("softmax"):
        posteriors, post_bf = posterior(core, scores, exchange(log_sum, "pose"))

    with jax.named_scope("gather_posteriors"):
        post = [lax.all_gather(post_bf, "grp", axis=0, axis_index_groups=z_groups)] + [None] * 3
        for d in (1, 3, 2):
            post[d] = lax.ppermute(post[0], "grp", grp_shift(d))
        post[0], own = lax.optimization_barrier((post[0], own))
        other = lax.ppermute(own, "pose", pose_shift(0, 0, 1))

    with jax.named_scope("back_project"):
        start = group * slab
        near, far, stacks = (0,), (1, 3, 2), (own, other)
        before = back_project(start, width, near, [post[d] for d in near], stacks, ahead=far)
        (back_proj,) = back_project(start, width, far, [post[d] for d in far], stacks, before=before)
    return (posteriors, back_proj)


def solution(mesh):
    placed = (
        P(None, "grp", None),
        P(None, "pose", "grp"),
        P("grp"),
        P(),
        P(),
        P("pose"),
        P("pose"),
        P("grp", None),
    )
    return jax.shard_map(
        on_device,
        mesh=mesh,
        in_specs=placed,
        out_specs=(P("grp", "pose"), P(None, "pose", "grp")),
        check_vma=False,
    )
```

```python
import functools
import math

import jax
import jax.numpy as jnp
from jax import lax
from jax.experimental import pallas as pl
from jax.experimental.pallas import tpu as pltpu
from jax.sharding import PartitionSpec as P

NEG_FILL = -1e30
NX, NZH = 4, 4
NY, NZL, NC = 4, 4, 2
LANES = 128
TERM_ROWS = 16
SCORE_VMEM = 53 << 20
SMALL_VMEM = 20 << 20
WEIGHT_VMEM = 60 << 20
SMALL_COST = pl.CostEstimate(flops=1, bytes_accessed=1, transcendentals=0)
INTERPRET = False


def grp_shift(dx):
    return [(x * NZH + z, ((x + dx) % NX) * NZH + z) for x in range(NX) for z in range(NZH)]


def pose_shift(dy, dz, dc):
    return [
        (
            (y * NZL + z) * NC + c,
            (((y + dy) % NY) * NZL + (z + dz) % NZL) * NC + (c + dc) % NC,
        )
        for y in range(NY)
        for z in range(NZL)
        for c in range(NC)
    ]


def share_pairs():
    n_pose = NY * NZL * NC
    pairs = []
    for x in range(NX):
        for zh in range(NZH):
            for y in range(NY):
                for zl in range(NZL):
                    for c in range(NC):
                        src = (x * NZH + zh) * n_pose + (y * NZL + zl) * NC + c
                        dst = (((x + y) % NX) * NZH + zl) * n_pose + (y * NZL + zh) * NC + c
                        pairs.append((src, dst))
    return pairs


SIN_TERMS = tuple(
    (-1) ** n * (2 * math.pi) ** (2 * n + 1) / math.factorial(2 * n + 1) for n in range(7)
)


def sin_quarter(t, scale=1.0):
    square = t * t
    value = square * (scale * SIN_TERMS[-1]) + scale * SIN_TERMS[-2]
    for term in SIN_TERMS[-3::-1]:
        value = value * square + scale * term
    return value * t


WEIGHT_ROWS = 32


def dot_nt(a, b):
    return lax.dot_general(a, b, (((1,), (1,)), ((), ())), preferred_element_type=jnp.float32)


def score_terms(proj, weighted_real, weighted_imag, noise):
    n_z = proj.shape[0]
    real = jnp.concatenate([proj[z, 0] for z in range(n_z)], axis=1)
    imag = jnp.concatenate([proj[z, 1] for z in range(n_z)], axis=1)
    real_f, imag_f = real.astype(jnp.float32), imag.astype(jnp.float32)
    power = (real_f * real_f + imag_f * imag_f).astype(jnp.bfloat16)
    return dot_nt(real, weighted_real) + dot_nt(imag, weighted_imag) - 0.5 * dot_nt(power, noise)


def weight_kernel(
    x_ref, images_hbm, sin_ref, cos_ref, inv_ref, proj_ref, weighted_hbm, noise_hbm, part_ref,
    images_ref, weighted_ref, noise_ref, sems,
):
    n, width = images_ref.shape[1:]
    steps = n // WEIGHT_ROWS

    def rows_of(i):
        return pl.ds(pl.multiple_of(i * WEIGHT_ROWS, WEIGHT_ROWS), WEIGHT_ROWS)

    def copy_in(i):
        rows = rows_of(i)
        return pltpu.make_async_copy(
            images_hbm.at[:, rows, :], images_ref.at[:, rows, :], sems.at[0, i]
        )

    def copies_out(i):
        rows = rows_of(i)
        return (
            pltpu.make_async_copy(
                weighted_ref.at[:, rows, :], weighted_hbm.at[:, rows, :], sems.at[1, i]
            ),
            pltpu.make_async_copy(noise_ref.at[rows, :], noise_hbm.at[rows, :], sems.at[2, i]),
        )

    def start(i, _):
        copy_in(i).start()
        return 0

    def body(i, _):
        copy_in(i).wait()
        rows = rows_of(i)
        sin_lo, cos_lo = sin_ref[rows, :LANES], cos_ref[rows, :LANES]
        sin_all, cos_all = sin_ref[rows, LANES:], cos_ref[rows, LANES:]
        for j in range(width // LANES):
            cols = slice(j * LANES, (j + 1) * LANES)
            contrast = -(sin_all[:, j : j + 1] * cos_lo + cos_all[:, j : j + 1] * sin_lo)
            scaled = contrast * inv_ref[:, cols]
            for c in range(2):
                image = images_ref[c, rows, cols].astype(jnp.float32)
                weighted_ref[c, rows, cols] = (image * scaled).astype(jnp.bfloat16)
            noise_ref[rows, cols] = (contrast * scaled).astype(jnp.bfloat16)
        for copy in copies_out(i):
            copy.start()
        return 0

    def finish(i, _):
        for copy in copies_out(i):
            copy.wait()
        return 0

    lax.fori_loop(0, steps, start, 0)
    lax.fori_loop(0, steps, body, 0)
    block = proj_ref.shape[0] * proj_ref.shape[3]
    cols = pl.ds(pl.multiple_of(x_ref[0] * block, block), block)
    part_ref[...] = score_terms(
        proj_ref, weighted_ref[0, :, cols], weighted_ref[1, :, cols], noise_ref[:, cols]
    )
    lax.fori_loop(0, steps, finish, 0)


def weight_images(x, images, defocus, inv_sigma2, proj):
    _, n, width = images.shape
    low = jnp.arange(LANES, dtype=jnp.float32) / width
    high = (jnp.arange(LANES, dtype=jnp.float32) * LANES + 0.5) / width
    phase = jnp.concatenate(
        [defocus[:, None] * low[None, :], defocus[:, None] * high[None, :] + 0.1], axis=1
    )
    assert width <= LANES * LANES
    in_hbm, in_vmem = pl.BlockSpec(memory_space=pl.ANY), pl.BlockSpec(memory_space=pltpu.VMEM)
    return pl.pallas_call(
        weight_kernel,
        in_specs=[pl.BlockSpec(memory_space=pltpu.SMEM), in_hbm] + [in_vmem] * 4,
        out_specs=[in_hbm, in_hbm, in_vmem],
        out_shape=[
            jax.ShapeDtypeStruct((2, n, width), jnp.bfloat16),
            jax.ShapeDtypeStruct((n, width), jnp.bfloat16),
            jax.ShapeDtypeStruct((proj.shape[2], n), jnp.float32),
        ],
        scratch_shapes=[
            pltpu.VMEM((2, n, width), jnp.bfloat16),
            pltpu.VMEM((2, n, width), jnp.bfloat16),
            pltpu.VMEM((n, width), jnp.bfloat16),
            pltpu.SemaphoreType.DMA((3, n // WEIGHT_ROWS)),
        ],
        cost_estimate=SMALL_COST,
        compiler_params=pltpu.CompilerParams(vmem_limit_bytes=WEIGHT_VMEM),
        interpret=INTERPRET,
        name="weight_images",
    )(x[None], images, jnp.sin(phase), jnp.cos(phase), inv_sigma2[None, :], proj)


def score_kernel(
    x_ref, proj_hbm, weighted_hbm, noise_hbm, part_hbm, bias_ref, scores_ref, log_sum_ref,
    proj_ref, weighted_ref, noise_ref, part_ref, sems, part_sem,
):
    n_s, n_z, _, _, slab = proj_ref.shape
    block = n_z * slab

    def copies(i):
        source = (x_ref[0] + i + 1) & (NX - 1)
        cols = pl.ds(pl.multiple_of(source * block, block), block)
        return (
            pltpu.make_async_copy(proj_hbm.at[source], proj_ref.at[i], sems.at[0, i]),
            pltpu.make_async_copy(weighted_hbm.at[:, :, cols], weighted_ref.at[i], sems.at[1, i]),
            pltpu.make_async_copy(noise_hbm.at[:, cols], noise_ref.at[i], sems.at[2, i]),
        )

    for i in range(n_s):
        for copy in copies(i):
            copy.start()
    part_copy = pltpu.make_async_copy(part_hbm, part_ref, part_sem)
    part_copy.start()
    total = None
    for i in range(n_s):
        for copy in copies(i):
            copy.wait()
        terms = score_terms(proj_ref.at[i], weighted_ref[i, 0], weighted_ref[i, 1], noise_ref[i])
        total = terms if total is None else total + terms
    part_copy.wait()
    total += part_ref[...]
    bias = bias_ref[...]
    scores = jnp.where(bias == NEG_FILL, bias, total + bias)
    scores_ref[...] = scores
    peak = jnp.max(scores, axis=0, keepdims=True)
    log_sum = peak + jnp.log(jnp.sum(jnp.exp(scores - peak), axis=0, keepdims=True))
    log_sum_ref[...] = jnp.broadcast_to(log_sum[None], log_sum_ref.shape)


def score(x, proj, weighted, noise, part, bias, copies):
    n_x, n_z, _, rows, slab = proj.shape
    n = weighted.shape[1]
    in_hbm, in_vmem = pl.BlockSpec(memory_space=pl.ANY), pl.BlockSpec(memory_space=pltpu.VMEM)
    return pl.pallas_call(
        score_kernel,
        in_specs=[pl.BlockSpec(memory_space=pltpu.SMEM)] + [in_hbm] * 4 + [in_vmem],
        out_specs=[in_vmem] * 2,
        out_shape=[
            jax.ShapeDtypeStruct((rows, n), jnp.float32),
            jax.ShapeDtypeStruct((copies, 1, n), jnp.float32),
        ],
        scratch_shapes=[
            pltpu.VMEM((n_x - 1,) + proj.shape[1:], jnp.bfloat16),
            pltpu.VMEM((n_x - 1, 2, n, n_z * slab), jnp.bfloat16),
            pltpu.VMEM((n_x - 1, n, n_z * slab), jnp.bfloat16),
            pltpu.VMEM((rows, n), jnp.float32),
            pltpu.SemaphoreType.DMA((3, n_x - 1)),
            pltpu.SemaphoreType.DMA,
        ],
        cost_estimate=SMALL_COST,
        compiler_params=pltpu.CompilerParams(vmem_limit_bytes=SCORE_VMEM),
        interpret=INTERPRET,
        name="score",
    )(x[None], proj, weighted, noise, part, bias)


def posterior_kernel(core_ref, scores_ref, log_sums_ref, post_ref, post_bf_ref):
    parts = log_sums_ref[...]
    peak = jnp.max(parts, axis=0)
    log_sum = peak + jnp.log(jnp.sum(jnp.exp(parts - peak[None]), axis=0))
    posteriors = jnp.exp(scores_ref[...] - log_sum)
    half = posteriors.shape[1] // NC
    swapped = jnp.concatenate([posteriors[:, half:], posteriors[:, :half]], axis=1)
    own_first = jnp.where(core_ref[0] == 0, posteriors, swapped).astype(jnp.bfloat16)
    post_bf_ref[...] = own_first
    post_ref[...] = posteriors.T


def posterior(core, scores, log_sums):
    rows, n = scores.shape
    return pl.pallas_call(
        posterior_kernel,
        in_specs=[
            pl.BlockSpec(memory_space=pltpu.SMEM),
            pl.BlockSpec(memory_space=pltpu.VMEM),
            pl.BlockSpec(memory_space=pltpu.VMEM),
        ],
        out_shape=[
            jax.ShapeDtypeStruct((n, rows), jnp.float32),
            jax.ShapeDtypeStruct((rows, n), jnp.bfloat16),
        ],
        cost_estimate=SMALL_COST,
        compiler_params=pltpu.CompilerParams(vmem_limit_bytes=SMALL_VMEM),
        interpret=INTERPRET,
        name="posterior",
    )(core[None], scores, log_sums)


def squared_contrast(defocus, freq2):
    turns = freq2 * (defocus * (1.0 / math.pi)) + 0.1 / math.pi
    return 0.5 - sin_quarter(0.25 - jnp.abs(turns - jnp.round(turns)), 0.5)


def defocus_terms(defocus):
    scaled = defocus * (1.0 / 256.0)
    first = lax.reduce_precision(scaled, 8, 7)
    second = lax.reduce_precision(scaled - first, 8, 7)
    third = scaled - first - second
    return jnp.stack([first, second, third]).astype(jnp.bfloat16)


def squares_of(stacks, freq2):
    parts = []
    half = freq2.shape[1]
    for stack in stacks:
        terms = stack.astype(jnp.float32)
        defocus = (terms[0:1, :half] + terms[1:2, :half] + terms[2:3, :half]) * 256.0
        parts.append(squared_contrast(defocus, freq2).astype(jnp.bfloat16))
    return jnp.concatenate(parts, axis=1)


def back_kernel(sources, ahead, width, start_ref, *refs):
    last = not ahead
    n_s = len(sources)
    posts, images = refs[:n_s], refs[n_s : n_s + 2]
    if last:
        before_ref, squares_ref, out_ref = refs[n_s + 2 :]
    else:
        out_ref, squares_ref = refs[n_s + 2 :]
    n_z, _, n = posts[0].shape
    slab, half = out_ref.shape[2], n // NC

    def stacked(source, first, size):
        rows = slice(first, first + size)
        return [ref[source, t, rows] for t in range(n_z) for ref in images]

    if not last:
        pixel = start_ref[0] + lax.broadcasted_iota(jnp.int32, (slab, half), 0)
        freq2 = (pixel.astype(jnp.float32) + 0.5) * (1.0 / width)
    for i, source in enumerate(sources):
        post = jnp.concatenate([posts[i][t] for t in range(n_z)], axis=1)
        for c in range(3):
            if c < 2:
                image = jnp.concatenate(stacked(source, c * half, half), axis=0)
                total = jnp.dot(post, image, preferred_element_type=jnp.float32)
            elif last:
                total = dot_nt(post, squares_ref[i])
            else:
                total = dot_nt(post, squares_of(stacked(source, n, TERM_ROWS), freq2))
            if i > 0:
                total += out_ref[c]
            elif last:
                total += before_ref[c]
            out_ref[c] = total
    for i, source in enumerate(ahead):
        squares_ref[i] = squares_of(stacked(source, n, TERM_ROWS), freq2)


def back_project(start, width, sources, posts, images, ahead=(), before=()):
    n_z, rows, n = posts[0].shape
    slab = images[0].shape[3]
    in_vmem = pl.BlockSpec(memory_space=pltpu.VMEM)
    out_shape = [jax.ShapeDtypeStruct((3, rows, slab), jnp.float32)]
    if ahead:
        out_shape.append(jax.ShapeDtypeStruct((len(ahead), slab, n_z * n), jnp.bfloat16))
    return pl.pallas_call(
        functools.partial(back_kernel, sources, ahead, width),
        in_specs=[pl.BlockSpec(memory_space=pltpu.SMEM)]
        + [in_vmem] * (len(sources) + 2 + len(before)),
        out_specs=[in_vmem] * len(out_shape),
        out_shape=out_shape,
        cost_estimate=SMALL_COST,
        compiler_params=pltpu.CompilerParams(vmem_limit_bytes=SMALL_VMEM),
        interpret=INTERPRET,
        name="back_project",
    )(start[None], *posts, *images, *before)


def exchange(copies, axis, groups=None):
    return lax.all_to_all(copies, axis, 0, 0, axis_index_groups=groups)


def copies_of(value, size):
    return jnp.broadcast_to(value[None], (size,) + value.shape)


def on_device(
    images, projections, defocus, inv_sigma2, log_prior, row_class, pose_block, significant
):
    _, n, width = images.shape
    _, rows, slab = projections.shape
    half = n // NC
    group, pose = lax.axis_index("grp"), lax.axis_index("pose")
    x = group >> 2
    y, zl, core = pose >> 3, (pose >> 1) & 3, pose & 1

    z_groups = [[a * NZH + b for b in range(NZH)] for a in range(NX)]
    x_groups = [[a * NZH + b for a in range(NX)] for b in range(NZH)]
    y_groups = [
        [(a * NZL + b) * NC + c for a in range(NY)] for b in range(NZL) for c in range(NC)
    ]
    with jax.named_scope("gather_projections"):
        proj_z = lax.all_gather(projections, "grp", axis=0, axis_index_groups=z_groups)
        proj_z, defocus = lax.optimization_barrier((proj_z, defocus))
        proj = lax.all_gather(proj_z, "grp", axis=0, axis_index_groups=x_groups)

    with jax.named_scope("exchange_images"):
        target = (((x + y) & 3) << 2) + zl
        cut = lax.dynamic_slice(images, (0, core * half, target * slab), (2, half, slab))
        part_defocus = lax.dynamic_slice(defocus, (core * half,), (half,))
        pixel = (target * slab + jnp.arange(slab)).astype(jnp.float32)
        contrast = -jnp.sin(part_defocus[:, None] * ((pixel + 0.5) / width)[None, :] + 0.1)
        cut = (cut.astype(jnp.float32) * contrast[None]).astype(jnp.bfloat16)
        terms = jnp.pad(defocus_terms(part_defocus), ((0, TERM_ROWS - 3), (0, slab - half)))
        share = jnp.concatenate([cut.reshape(2 * half, slab), terms], axis=0)
        share = lax.ppermute(share, ("grp", "pose"), share_pairs())

    with jax.named_scope("weights"):
        weighted, noise, part = weight_images(x, images, defocus, inv_sigma2, proj_z)
        class_match = row_class[:, None] == jnp.arange(log_prior.shape[0])[None, :]
        prior_rows = jnp.sum(jnp.where(class_match, log_prior[None, :], 0.0), axis=1)
        block_table = pose_block[:, None] == jnp.arange(significant.shape[1])[None, :]
        hits = jnp.einsum(
            "rb,ib->ri",
            block_table.astype(jnp.bfloat16),
            significant.astype(jnp.bfloat16),
            preferred_element_type=jnp.float32,
        )
        bias = jnp.where(hits > 0.5, prior_rows[:, None], jnp.float32(NEG_FILL))

    with jax.named_scope("gather_images"):
        share, part, bias = lax.optimization_barrier((share, part, bias))
        turned = copies_of(share, NZL)
        for d in (1, 2, 3):
            block = lax.ppermute(share, "pose", pose_shift(0, d, 0))
            turned = lax.dynamic_update_slice_in_dim(turned, block[None], (zl - d) & 3, 0)
        turned, proj = lax.optimization_barrier((turned, proj))
        own = lax.all_gather(turned, "pose", axis=0, axis_index_groups=y_groups)

    with jax.named_scope("scores"):
        scores, log_sum = score(x, proj, weighted, noise, part, bias, NY * NZL * NC)

    with jax.named_scope("softmax"):
        posteriors, post_bf = posterior(core, scores, exchange(log_sum, "pose"))

    with jax.named_scope("gather_posteriors"):
        post = [lax.all_gather(post_bf, "grp", axis=0, axis_index_groups=z_groups)] + [None] * 3
        for d in (2, 1, 3):
            post[d] = lax.ppermute(post[0], "grp", grp_shift(d))
        post[0], own = lax.optimization_barrier((post[0], own))
        other = lax.ppermute(own, "pose", pose_shift(0, 0, 1))

    with jax.named_scope("back_project"):
        start = group * slab
        near, far, stacks = (0,), (1, 2, 3), (own, other)
        before = back_project(start, width, near, [post[d] for d in near], stacks, ahead=far)
        (back_proj,) = back_project(start, width, far, [post[d] for d in far], stacks, before=before)
    return (posteriors, back_proj)


def solution(mesh):
    placed = (
        P(None, "grp", None),
        P(None, "pose", "grp"),
        P("grp"),
        P(),
        P(),
        P("pose"),
        P("pose"),
        P("grp", None),
    )
    return jax.shard_map(
        on_device,
        mesh=mesh,
        in_specs=placed,
        out_specs=(P("grp", "pose"), P(None, "pose", "grp")),
        check_vma=False,
    )
```

```python
import functools
import math

import jax
import jax.numpy as jnp
from jax import lax
from jax.experimental import pallas as pl
from jax.experimental.pallas import tpu as pltpu
from jax.sharding import PartitionSpec as P

NEG_FILL = -1e30
NX, NZH = 4, 4
NY, NZL, NC = 4, 4, 2
LANES = 128
TERM_ROWS = 16
SCORE_VMEM = 53 << 20
SMALL_VMEM = 20 << 20
WEIGHT_VMEM = 60 << 20
SMALL_COST = pl.CostEstimate(flops=1, bytes_accessed=1, transcendentals=0)
INTERPRET = False


def grp_shift(dx):
    return [(x * NZH + z, ((x + dx) % NX) * NZH + z) for x in range(NX) for z in range(NZH)]


def pose_shift(dy, dz, dc):
    return [
        (
            (y * NZL + z) * NC + c,
            (((y + dy) % NY) * NZL + (z + dz) % NZL) * NC + (c + dc) % NC,
        )
        for y in range(NY)
        for z in range(NZL)
        for c in range(NC)
    ]


def share_pairs():
    n_pose = NY * NZL * NC
    pairs = []
    for x in range(NX):
        for zh in range(NZH):
            for y in range(NY):
                for zl in range(NZL):
                    for c in range(NC):
                        src = (x * NZH + zh) * n_pose + (y * NZL + zl) * NC + c
                        dst = (((x + y) % NX) * NZH + zl) * n_pose + (y * NZL + zh) * NC + c
                        pairs.append((src, dst))
    return pairs


SIN_TERMS = tuple(
    (-1) ** n * (2 * math.pi) ** (2 * n + 1) / math.factorial(2 * n + 1) for n in range(7)
)


def sin_quarter(t, scale=1.0):
    square = t * t
    value = square * (scale * SIN_TERMS[-1]) + scale * SIN_TERMS[-2]
    for term in SIN_TERMS[-3::-1]:
        value = value * square + scale * term
    return value * t


WEIGHT_ROWS = 32


def dot_nt(a, b):
    return lax.dot_general(a, b, (((1,), (1,)), ((), ())), preferred_element_type=jnp.float32)


def score_terms(proj, weighted_real, weighted_imag, noise):
    n_z = proj.shape[0]
    real = jnp.concatenate([proj[z, 0] for z in range(n_z)], axis=1)
    imag = jnp.concatenate([proj[z, 1] for z in range(n_z)], axis=1)
    real_f, imag_f = real.astype(jnp.float32), imag.astype(jnp.float32)
    power = (real_f * real_f + imag_f * imag_f).astype(jnp.bfloat16)
    return dot_nt(real, weighted_real) + dot_nt(imag, weighted_imag) - 0.5 * dot_nt(power, noise)


def weight_kernel(
    x_ref, images_hbm, sin_ref, cos_ref, inv_ref, proj_ref, weighted_hbm, noise_hbm, part_ref,
    images_ref, weighted_ref, noise_ref, sems,
):
    n, width = images_ref.shape[1:]
    steps = n // WEIGHT_ROWS

    def rows_of(i):
        return pl.ds(pl.multiple_of(i * WEIGHT_ROWS, WEIGHT_ROWS), WEIGHT_ROWS)

    def copy_in(i):
        rows = rows_of(i)
        return pltpu.make_async_copy(
            images_hbm.at[:, rows, :], images_ref.at[:, rows, :], sems.at[0, i]
        )

    def copies_out(i):
        rows = rows_of(i)
        return (
            pltpu.make_async_copy(
                weighted_ref.at[:, rows, :], weighted_hbm.at[:, rows, :], sems.at[1, i]
            ),
            pltpu.make_async_copy(noise_ref.at[rows, :], noise_hbm.at[rows, :], sems.at[2, i]),
        )

    def start(i, _):
        copy_in(i).start()
        return 0

    def body(i, _):
        copy_in(i).wait()
        rows = rows_of(i)
        sin_lo, cos_lo = sin_ref[rows, :LANES], cos_ref[rows, :LANES]
        sin_all, cos_all = sin_ref[rows, LANES:], cos_ref[rows, LANES:]
        for j in range(width // LANES):
            cols = slice(j * LANES, (j + 1) * LANES)
            contrast = -(sin_all[:, j : j + 1] * cos_lo + cos_all[:, j : j + 1] * sin_lo)
            scaled = contrast * inv_ref[:, cols]
            for c in range(2):
                image = images_ref[c, rows, cols].astype(jnp.float32)
                weighted_ref[c, rows, cols] = (image * scaled).astype(jnp.bfloat16)
            noise_ref[rows, cols] = (contrast * scaled).astype(jnp.bfloat16)
        for copy in copies_out(i):
            copy.start()
        return 0

    def finish(i, _):
        for copy in copies_out(i):
            copy.wait()
        return 0

    lax.fori_loop(0, steps, start, 0)
    lax.fori_loop(0, steps, body, 0)
    block = proj_ref.shape[0] * proj_ref.shape[3]
    cols = pl.ds(pl.multiple_of(x_ref[0] * block, block), block)
    part_ref[...] = score_terms(
        proj_ref, weighted_ref[0, :, cols], weighted_ref[1, :, cols], noise_ref[:, cols]
    )
    lax.fori_loop(0, steps, finish, 0)


def weight_images(x, images, defocus, inv_sigma2, proj):
    _, n, width = images.shape
    low = jnp.arange(LANES, dtype=jnp.float32) / width
    high = (jnp.arange(LANES, dtype=jnp.float32) * LANES + 0.5) / width
    phase = jnp.concatenate(
        [defocus[:, None] * low[None, :], defocus[:, None] * high[None, :] + 0.1], axis=1
    )
    assert width <= LANES * LANES
    in_hbm, in_vmem = pl.BlockSpec(memory_space=pl.ANY), pl.BlockSpec(memory_space=pltpu.VMEM)
    return pl.pallas_call(
        weight_kernel,
        in_specs=[pl.BlockSpec(memory_space=pltpu.SMEM), in_hbm] + [in_vmem] * 4,
        out_specs=[in_hbm, in_hbm, in_vmem],
        out_shape=[
            jax.ShapeDtypeStruct((2, n, width), jnp.bfloat16),
            jax.ShapeDtypeStruct((n, width), jnp.bfloat16),
            jax.ShapeDtypeStruct((proj.shape[2], n), jnp.float32),
        ],
        scratch_shapes=[
            pltpu.VMEM((2, n, width), jnp.bfloat16),
            pltpu.VMEM((2, n, width), jnp.bfloat16),
            pltpu.VMEM((n, width), jnp.bfloat16),
            pltpu.SemaphoreType.DMA((3, n // WEIGHT_ROWS)),
        ],
        cost_estimate=SMALL_COST,
        compiler_params=pltpu.CompilerParams(vmem_limit_bytes=WEIGHT_VMEM),
        interpret=INTERPRET,
        name="weight_images",
    )(x[None], images, jnp.sin(phase), jnp.cos(phase), inv_sigma2[None, :], proj)


def score_kernel(
    x_ref, proj_hbm, weighted_hbm, noise_hbm, part_hbm, bias_ref, scores_ref, log_sum_ref,
    proj_ref, weighted_ref, noise_ref, part_ref, sems, part_sem,
):
    n_s, n_z, _, _, slab = proj_ref.shape
    block = n_z * slab

    def copies(i):
        source = (x_ref[0] + i + 1) & (NX - 1)
        cols = pl.ds(pl.multiple_of(source * block, block), block)
        return (
            pltpu.make_async_copy(proj_hbm.at[source], proj_ref.at[i], sems.at[0, i]),
            pltpu.make_async_copy(weighted_hbm.at[:, :, cols], weighted_ref.at[i], sems.at[1, i]),
            pltpu.make_async_copy(noise_hbm.at[:, cols], noise_ref.at[i], sems.at[2, i]),
        )

    for i in range(n_s):
        for copy in copies(i):
            copy.start()
    part_copy = pltpu.make_async_copy(part_hbm, part_ref, part_sem)
    part_copy.start()
    total = None
    for i in range(n_s):
        for copy in copies(i):
            copy.wait()
        terms = score_terms(proj_ref.at[i], weighted_ref[i, 0], weighted_ref[i, 1], noise_ref[i])
        total = terms if total is None else total + terms
    part_copy.wait()
    total += part_ref[...]
    bias = bias_ref[...]
    scores = jnp.where(bias == NEG_FILL, bias, total + bias)
    scores_ref[...] = scores
    peak = jnp.max(scores, axis=0, keepdims=True)
    log_sum = peak + jnp.log(jnp.sum(jnp.exp(scores - peak), axis=0, keepdims=True))
    log_sum_ref[...] = jnp.broadcast_to(log_sum[None], log_sum_ref.shape)


def score(x, proj, weighted, noise, part, bias, copies):
    n_x, n_z, _, rows, slab = proj.shape
    n = weighted.shape[1]
    in_hbm, in_vmem = pl.BlockSpec(memory_space=pl.ANY), pl.BlockSpec(memory_space=pltpu.VMEM)
    return pl.pallas_call(
        score_kernel,
        in_specs=[pl.BlockSpec(memory_space=pltpu.SMEM)] + [in_hbm] * 4 + [in_vmem],
        out_specs=[in_vmem] * 2,
        out_shape=[
            jax.ShapeDtypeStruct((rows, n), jnp.float32),
            jax.ShapeDtypeStruct((copies, 1, n), jnp.float32),
        ],
        scratch_shapes=[
            pltpu.VMEM((n_x - 1,) + proj.shape[1:], jnp.bfloat16),
            pltpu.VMEM((n_x - 1, 2, n, n_z * slab), jnp.bfloat16),
            pltpu.VMEM((n_x - 1, n, n_z * slab), jnp.bfloat16),
            pltpu.VMEM((rows, n), jnp.float32),
            pltpu.SemaphoreType.DMA((3, n_x - 1)),
            pltpu.SemaphoreType.DMA,
        ],
        cost_estimate=SMALL_COST,
        compiler_params=pltpu.CompilerParams(vmem_limit_bytes=SCORE_VMEM),
        interpret=INTERPRET,
        name="score",
    )(x[None], proj, weighted, noise, part, bias)


def posterior_kernel(core_ref, scores_ref, log_sums_ref, post_ref, post_bf_ref):
    parts = log_sums_ref[...]
    peak = jnp.max(parts, axis=0)
    log_sum = peak + jnp.log(jnp.sum(jnp.exp(parts - peak[None]), axis=0))
    posteriors = jnp.exp(scores_ref[...] - log_sum)
    half = posteriors.shape[1] // NC
    swapped = jnp.concatenate([posteriors[:, half:], posteriors[:, :half]], axis=1)
    own_first = jnp.where(core_ref[0] == 0, posteriors, swapped).astype(jnp.bfloat16)
    post_bf_ref[...] = own_first
    post_ref[...] = posteriors.T


def posterior(core, scores, log_sums):
    rows, n = scores.shape
    return pl.pallas_call(
        posterior_kernel,
        in_specs=[
            pl.BlockSpec(memory_space=pltpu.SMEM),
            pl.BlockSpec(memory_space=pltpu.VMEM),
            pl.BlockSpec(memory_space=pltpu.VMEM),
        ],
        out_shape=[
            jax.ShapeDtypeStruct((n, rows), jnp.float32),
            jax.ShapeDtypeStruct((rows, n), jnp.bfloat16),
        ],
        cost_estimate=SMALL_COST,
        compiler_params=pltpu.CompilerParams(vmem_limit_bytes=SMALL_VMEM),
        interpret=INTERPRET,
        name="posterior",
    )(core[None], scores, log_sums)


def squared_contrast(defocus, freq2):
    turns = freq2 * (defocus * (1.0 / math.pi)) + 0.1 / math.pi
    return 0.5 - sin_quarter(0.25 - jnp.abs(turns - jnp.round(turns)), 0.5)


def defocus_terms(defocus):
    scaled = defocus * (1.0 / 256.0)
    first = lax.reduce_precision(scaled, 8, 7)
    second = lax.reduce_precision(scaled - first, 8, 7)
    third = scaled - first - second
    return jnp.stack([first, second, third]).astype(jnp.bfloat16)


def squares_of(stacks, freq2):
    parts = []
    half = freq2.shape[1]
    for stack in stacks:
        terms = stack.astype(jnp.float32)
        defocus = (terms[0:1, :half] + terms[1:2, :half] + terms[2:3, :half]) * 256.0
        parts.append(squared_contrast(defocus, freq2).astype(jnp.bfloat16))
    return jnp.concatenate(parts, axis=1)


def back_kernel(sources, ahead, width, start_ref, *refs):
    last = not ahead
    n_s = len(sources)
    posts, images = refs[:n_s], refs[n_s : n_s + 2]
    if last:
        before_ref, squares_ref, out_ref = refs[n_s + 2 :]
    else:
        out_ref, squares_ref = refs[n_s + 2 :]
    n_z, _, n = posts[0].shape
    slab, half = out_ref.shape[2], n // NC

    def stacked(source, first, size):
        rows = slice(first, first + size)
        return [ref[source, t, rows] for t in range(n_z) for ref in images]

    if not last:
        pixel = start_ref[0] + lax.broadcasted_iota(jnp.int32, (slab, half), 0)
        freq2 = (pixel.astype(jnp.float32) + 0.5) * (1.0 / width)
    for i, source in enumerate(sources):
        post = jnp.concatenate([posts[i][t] for t in range(n_z)], axis=1)
        for c in range(3):
            if c < 2:
                image = jnp.concatenate(stacked(source, c * half, half), axis=0)
                total = jnp.dot(post, image, preferred_element_type=jnp.float32)
            elif last:
                total = dot_nt(post, squares_ref[i])
            else:
                total = dot_nt(post, squares_of(stacked(source, n, TERM_ROWS), freq2))
            if i > 0:
                total += out_ref[c]
            elif last:
                total += before_ref[c]
            out_ref[c] = total
    for i, source in enumerate(ahead):
        squares_ref[i] = squares_of(stacked(source, n, TERM_ROWS), freq2)


def back_project(start, width, sources, posts, images, ahead=(), before=()):
    n_z, rows, n = posts[0].shape
    slab = images[0].shape[3]
    in_vmem = pl.BlockSpec(memory_space=pltpu.VMEM)
    out_shape = [jax.ShapeDtypeStruct((3, rows, slab), jnp.float32)]
    if ahead:
        out_shape.append(jax.ShapeDtypeStruct((len(ahead), slab, n_z * n), jnp.bfloat16))
    return pl.pallas_call(
        functools.partial(back_kernel, sources, ahead, width),
        in_specs=[pl.BlockSpec(memory_space=pltpu.SMEM)]
        + [in_vmem] * (len(sources) + 2 + len(before)),
        out_specs=[in_vmem] * len(out_shape),
        out_shape=out_shape,
        cost_estimate=SMALL_COST,
        compiler_params=pltpu.CompilerParams(vmem_limit_bytes=SMALL_VMEM),
        interpret=INTERPRET,
        name="back_project",
    )(start[None], *posts, *images, *before)


def exchange(copies, axis, groups=None):
    return lax.all_to_all(copies, axis, 0, 0, axis_index_groups=groups)


def copies_of(value, size):
    return jnp.broadcast_to(value[None], (size,) + value.shape)


def on_device(
    images, projections, defocus, inv_sigma2, log_prior, row_class, pose_block, significant
):
    _, n, width = images.shape
    _, rows, slab = projections.shape
    half = n // NC
    group, pose = lax.axis_index("grp"), lax.axis_index("pose")
    x = group >> 2
    y, zl, core = pose >> 3, (pose >> 1) & 3, pose & 1

    z_groups = [[a * NZH + b for b in range(NZH)] for a in range(NX)]
    x_groups = [[a * NZH + b for a in range(NX)] for b in range(NZH)]
    y_groups = [
        [(a * NZL + b) * NC + c for a in range(NY)] for b in range(NZL) for c in range(NC)
    ]
    with jax.named_scope("gather_projections"):
        proj_z = lax.all_gather(projections, "grp", axis=0, axis_index_groups=z_groups)
        proj_z, defocus = lax.optimization_barrier((proj_z, defocus))
        proj = lax.all_gather(proj_z, "grp", axis=0, axis_index_groups=x_groups)

    with jax.named_scope("exchange_images"):
        target = (((x + y) & 3) << 2) + zl
        cut = lax.dynamic_slice(images, (0, core * half, target * slab), (2, half, slab))
        part_defocus = lax.dynamic_slice(defocus, (core * half,), (half,))
        pixel = (target * slab + jnp.arange(slab)).astype(jnp.float32)
        contrast = -jnp.sin(part_defocus[:, None] * ((pixel + 0.5) / width)[None, :] + 0.1)
        cut = (cut.astype(jnp.float32) * contrast[None]).astype(jnp.bfloat16)
        terms = jnp.pad(defocus_terms(part_defocus), ((0, TERM_ROWS - 3), (0, slab - half)))
        share = jnp.concatenate([cut.reshape(2 * half, slab), terms], axis=0)
        share = lax.ppermute(share, ("grp", "pose"), share_pairs())

    with jax.named_scope("weights"):
        weighted, noise, part = weight_images(x, images, defocus, inv_sigma2, proj_z)
        class_match = row_class[:, None] == jnp.arange(log_prior.shape[0])[None, :]
        prior_rows = jnp.sum(jnp.where(class_match, log_prior[None, :], 0.0), axis=1)
        block_table = pose_block[:, None] == jnp.arange(significant.shape[1])[None, :]
        hits = jnp.einsum(
            "rb,ib->ri",
            block_table.astype(jnp.bfloat16),
            significant.astype(jnp.bfloat16),
            preferred_element_type=jnp.float32,
        )
        bias = jnp.where(hits > 0.5, prior_rows[:, None], jnp.float32(NEG_FILL))

    with jax.named_scope("gather_images"):
        share, part, bias = lax.optimization_barrier((share, part, bias))
        turned = copies_of(share, NZL)
        for d in (1, 2, 3):
            block = lax.ppermute(share, "pose", pose_shift(0, d, 0))
            turned = lax.dynamic_update_slice_in_dim(turned, block[None], (zl - d) & 3, 0)
        turned, proj = lax.optimization_barrier((turned, proj))
        own = lax.all_gather(turned, "pose", axis=0, axis_index_groups=y_groups)

    with jax.named_scope("scores"):
        scores, log_sum = score(x, proj, weighted, noise, part, bias, NY * NZL * NC)

    with jax.named_scope("softmax"):
        posteriors, post_bf = posterior(core, scores, exchange(log_sum, "pose"))

    with jax.named_scope("gather_posteriors"):
        post = [lax.all_gather(post_bf, "grp", axis=0, axis_index_groups=z_groups)] + [None] * 3
        for d in (1, 3, 2):
            post[d] = lax.ppermute(post[0], "grp", grp_shift(d))
        post[0], own = lax.optimization_barrier((post[0], own))
        other = lax.ppermute(own, "pose", pose_shift(0, 0, 1))

    with jax.named_scope("back_project"):
        start = group * slab
        near, far, stacks = (0,), (1, 3, 2), (own, other)
        before = back_project(start, width, near, [post[d] for d in near], stacks, ahead=far)
        (back_proj,) = back_project(start, width, far, [post[d] for d in far], stacks, before=before)
    return (posteriors, back_proj)


def solution(mesh):
    placed = (
        P(None, "grp", None),
        P(None, "pose", "grp"),
        P("grp"),
        P(),
        P(),
        P("pose"),
        P("pose"),
        P("grp", None),
    )
    return jax.shard_map(
        on_device,
        mesh=mesh,
        in_specs=placed,
        out_specs=(P("grp", "pose"), P(None, "pose", "grp")),
        check_vma=False,
    )
```

```python
import functools
import math

import jax
import jax.numpy as jnp
from jax import lax
from jax.experimental import pallas as pl
from jax.experimental.pallas import tpu as pltpu
from jax.sharding import PartitionSpec as P

NEG_FILL = -1e30
NX, NZH = 4, 4
NY, NZL, NC = 4, 4, 2
LANES = 128
TERM_ROWS = 16
SCORE_VMEM = 53 << 20
SMALL_VMEM = 20 << 20
WEIGHT_VMEM = 60 << 20
SMALL_COST = pl.CostEstimate(flops=1, bytes_accessed=1, transcendentals=0)
INTERPRET = False


def grp_shift(dx):
    return [(x * NZH + z, ((x + dx) % NX) * NZH + z) for x in range(NX) for z in range(NZH)]


def pose_shift(dy, dz, dc):
    return [
        (
            (y * NZL + z) * NC + c,
            (((y + dy) % NY) * NZL + (z + dz) % NZL) * NC + (c + dc) % NC,
        )
        for y in range(NY)
        for z in range(NZL)
        for c in range(NC)
    ]


def share_pairs():
    n_pose = NY * NZL * NC
    pairs = []
    for x in range(NX):
        for zh in range(NZH):
            for y in range(NY):
                for zl in range(NZL):
                    for c in range(NC):
                        src = (x * NZH + zh) * n_pose + (y * NZL + zl) * NC + c
                        dst = (((x + y) % NX) * NZH + zl) * n_pose + (y * NZL + zh) * NC + c
                        pairs.append((src, dst))
    return pairs


SIN_TERMS = tuple(
    (-1) ** n * (2 * math.pi) ** (2 * n + 1) / math.factorial(2 * n + 1) for n in range(7)
)


def sin_quarter(t, scale=1.0):
    square = t * t
    value = square * (scale * SIN_TERMS[-1]) + scale * SIN_TERMS[-2]
    for term in SIN_TERMS[-3::-1]:
        value = value * square + scale * term
    return value * t


WEIGHT_ROWS = 32


def dot_nt(a, b):
    return lax.dot_general(a, b, (((1,), (1,)), ((), ())), preferred_element_type=jnp.float32)


def score_terms(proj, weighted_real, weighted_imag, noise):
    n_z = proj.shape[0]
    real = jnp.concatenate([proj[z, 0] for z in range(n_z)], axis=1)
    imag = jnp.concatenate([proj[z, 1] for z in range(n_z)], axis=1)
    real_f, imag_f = real.astype(jnp.float32), imag.astype(jnp.float32)
    power = (real_f * real_f + imag_f * imag_f).astype(jnp.bfloat16)
    return dot_nt(real, weighted_real) + dot_nt(imag, weighted_imag) - 0.5 * dot_nt(power, noise)


def weight_kernel(
    x_ref, images_hbm, sin_ref, cos_ref, inv_ref, proj_ref, weighted_hbm, noise_hbm, part_ref,
    images_ref, weighted_ref, noise_ref, sems,
):
    n, width = images_ref.shape[1:]
    steps = n // WEIGHT_ROWS

    def rows_of(i):
        return pl.ds(pl.multiple_of(i * WEIGHT_ROWS, WEIGHT_ROWS), WEIGHT_ROWS)

    def copy_in(i):
        rows = rows_of(i)
        return pltpu.make_async_copy(
            images_hbm.at[:, rows, :], images_ref.at[:, rows, :], sems.at[0, i]
        )

    def copies_out(i):
        rows = rows_of(i)
        return (
            pltpu.make_async_copy(
                weighted_ref.at[:, rows, :], weighted_hbm.at[:, rows, :], sems.at[1, i]
            ),
            pltpu.make_async_copy(noise_ref.at[rows, :], noise_hbm.at[rows, :], sems.at[2, i]),
        )

    def start(i, _):
        copy_in(i).start()
        return 0

    def body(i, _):
        copy_in(i).wait()
        rows = rows_of(i)
        sin_lo, cos_lo = sin_ref[rows, :LANES], cos_ref[rows, :LANES]
        sin_all, cos_all = sin_ref[rows, LANES:], cos_ref[rows, LANES:]
        for j in range(width // LANES):
            cols = slice(j * LANES, (j + 1) * LANES)
            contrast = -(sin_all[:, j : j + 1] * cos_lo + cos_all[:, j : j + 1] * sin_lo)
            scaled = contrast * inv_ref[:, cols]
            for c in range(2):
                image = images_ref[c, rows, cols].astype(jnp.float32)
                weighted_ref[c, rows, cols] = (image * scaled).astype(jnp.bfloat16)
            noise_ref[rows, cols] = (contrast * scaled).astype(jnp.bfloat16)
        for copy in copies_out(i):
            copy.start()
        return 0

    def finish(i, _):
        for copy in copies_out(i):
            copy.wait()
        return 0

    lax.fori_loop(0, steps, start, 0)
    lax.fori_loop(0, steps, body, 0)
    block = proj_ref.shape[0] * proj_ref.shape[3]
    cols = pl.ds(pl.multiple_of(x_ref[0] * block, block), block)
    part_ref[...] = score_terms(
        proj_ref, weighted_ref[0, :, cols], weighted_ref[1, :, cols], noise_ref[:, cols]
    )
    lax.fori_loop(0, steps, finish, 0)


def weight_images(x, images, defocus, inv_sigma2, proj):
    _, n, width = images.shape
    low = jnp.arange(LANES, dtype=jnp.float32) / width
    high = (jnp.arange(LANES, dtype=jnp.float32) * LANES + 0.5) / width
    phase = jnp.concatenate(
        [defocus[:, None] * low[None, :], defocus[:, None] * high[None, :] + 0.1], axis=1
    )
    assert width <= LANES * LANES
    in_hbm, in_vmem = pl.BlockSpec(memory_space=pl.ANY), pl.BlockSpec(memory_space=pltpu.VMEM)
    return pl.pallas_call(
        weight_kernel,
        in_specs=[pl.BlockSpec(memory_space=pltpu.SMEM), in_hbm] + [in_vmem] * 4,
        out_specs=[in_hbm, in_hbm, in_vmem],
        out_shape=[
            jax.ShapeDtypeStruct((2, n, width), jnp.bfloat16),
            jax.ShapeDtypeStruct((n, width), jnp.bfloat16),
            jax.ShapeDtypeStruct((proj.shape[2], n), jnp.float32),
        ],
        scratch_shapes=[
            pltpu.VMEM((2, n, width), jnp.bfloat16),
            pltpu.VMEM((2, n, width), jnp.bfloat16),
            pltpu.VMEM((n, width), jnp.bfloat16),
            pltpu.SemaphoreType.DMA((3, n // WEIGHT_ROWS)),
        ],
        cost_estimate=SMALL_COST,
        compiler_params=pltpu.CompilerParams(vmem_limit_bytes=WEIGHT_VMEM),
        interpret=INTERPRET,
        name="weight_images",
    )(x[None], images, jnp.sin(phase), jnp.cos(phase), inv_sigma2[None, :], proj)


def score_kernel(
    x_ref, proj_hbm, weighted_hbm, noise_hbm, part_hbm, bias_ref, scores_ref, log_sum_ref,
    proj_ref, weighted_ref, noise_ref, part_ref, sems, part_sem,
):
    n_s, n_z, _, _, slab = proj_ref.shape
    block = n_z * slab

    def copies(i):
        source = (x_ref[0] + i + 1) & (NX - 1)
        cols = pl.ds(pl.multiple_of(source * block, block), block)
        return (
            pltpu.make_async_copy(proj_hbm.at[source], proj_ref.at[i], sems.at[0, i]),
            pltpu.make_async_copy(weighted_hbm.at[:, :, cols], weighted_ref.at[i], sems.at[1, i]),
            pltpu.make_async_copy(noise_hbm.at[:, cols], noise_ref.at[i], sems.at[2, i]),
        )

    for i in range(n_s):
        for copy in copies(i):
            copy.start()
    part_copy = pltpu.make_async_copy(part_hbm, part_ref, part_sem)
    part_copy.start()
    total = None
    for i in range(n_s):
        for copy in copies(i):
            copy.wait()
        terms = score_terms(proj_ref.at[i], weighted_ref[i, 0], weighted_ref[i, 1], noise_ref[i])
        total = terms if total is None else total + terms
    part_copy.wait()
    total += part_ref[...]
    bias = bias_ref[...]
    scores = jnp.where(bias == NEG_FILL, bias, total + bias)
    scores_ref[...] = scores
    peak = jnp.max(scores, axis=0, keepdims=True)
    log_sum = peak + jnp.log(jnp.sum(jnp.exp(scores - peak), axis=0, keepdims=True))
    log_sum_ref[...] = jnp.broadcast_to(log_sum[None], log_sum_ref.shape)


def score(x, proj, weighted, noise, part, bias, copies):
    n_x, n_z, _, rows, slab = proj.shape
    n = weighted.shape[1]
    in_hbm, in_vmem = pl.BlockSpec(memory_space=pl.ANY), pl.BlockSpec(memory_space=pltpu.VMEM)
    return pl.pallas_call(
        score_kernel,
        in_specs=[pl.BlockSpec(memory_space=pltpu.SMEM)] + [in_hbm] * 4 + [in_vmem],
        out_specs=[in_vmem] * 2,
        out_shape=[
            jax.ShapeDtypeStruct((rows, n), jnp.float32),
            jax.ShapeDtypeStruct((copies, 1, n), jnp.float32),
        ],
        scratch_shapes=[
            pltpu.VMEM((n_x - 1,) + proj.shape[1:], jnp.bfloat16),
            pltpu.VMEM((n_x - 1, 2, n, n_z * slab), jnp.bfloat16),
            pltpu.VMEM((n_x - 1, n, n_z * slab), jnp.bfloat16),
            pltpu.VMEM((rows, n), jnp.float32),
            pltpu.SemaphoreType.DMA((3, n_x - 1)),
            pltpu.SemaphoreType.DMA,
        ],
        cost_estimate=SMALL_COST,
        compiler_params=pltpu.CompilerParams(vmem_limit_bytes=SCORE_VMEM),
        interpret=INTERPRET,
        name="score",
    )(x[None], proj, weighted, noise, part, bias)


def posterior_kernel(core_ref, scores_ref, log_sums_ref, post_ref, post_bf_ref):
    parts = log_sums_ref[...]
    peak = jnp.max(parts, axis=0)
    log_sum = peak + jnp.log(jnp.sum(jnp.exp(parts - peak[None]), axis=0))
    posteriors = jnp.exp(scores_ref[...] - log_sum)
    half = posteriors.shape[1] // NC
    swapped = jnp.concatenate([posteriors[:, half:], posteriors[:, :half]], axis=1)
    own_first = jnp.where(core_ref[0] == 0, posteriors, swapped).astype(jnp.bfloat16)
    post_bf_ref[...] = own_first
    post_ref[...] = posteriors.T


def posterior(core, scores, log_sums):
    rows, n = scores.shape
    return pl.pallas_call(
        posterior_kernel,
        in_specs=[
            pl.BlockSpec(memory_space=pltpu.SMEM),
            pl.BlockSpec(memory_space=pltpu.VMEM),
            pl.BlockSpec(memory_space=pltpu.VMEM),
        ],
        out_shape=[
            jax.ShapeDtypeStruct((n, rows), jnp.float32),
            jax.ShapeDtypeStruct((rows, n), jnp.bfloat16),
        ],
        cost_estimate=SMALL_COST,
        compiler_params=pltpu.CompilerParams(vmem_limit_bytes=SMALL_VMEM),
        interpret=INTERPRET,
        name="posterior",
    )(core[None], scores, log_sums)


def squared_contrast(defocus, freq2):
    turns = freq2 * (defocus * (1.0 / math.pi)) + 0.1 / math.pi
    return 0.5 - sin_quarter(0.25 - jnp.abs(turns - jnp.round(turns)), 0.5)


def defocus_terms(defocus):
    scaled = defocus * (1.0 / 256.0)
    first = lax.reduce_precision(scaled, 8, 7)
    second = lax.reduce_precision(scaled - first, 8, 7)
    third = scaled - first - second
    return jnp.stack([first, second, third]).astype(jnp.bfloat16)


def squares_of(stacks, freq2):
    parts = []
    half = freq2.shape[1]
    for stack in stacks:
        terms = stack.astype(jnp.float32)
        defocus = (terms[0:1, :half] + terms[1:2, :half] + terms[2:3, :half]) * 256.0
        parts.append(squared_contrast(defocus, freq2).astype(jnp.bfloat16))
    return jnp.concatenate(parts, axis=1)


def back_kernel(sources, ahead, width, start_ref, *refs):
    last = not ahead
    n_s = len(sources)
    posts, images = refs[:n_s], refs[n_s : n_s + 2]
    if last:
        before_ref, squares_ref, out_ref = refs[n_s + 2 :]
    else:
        out_ref, squares_ref = refs[n_s + 2 :]
    n_z, _, n = posts[0].shape
    slab, half = out_ref.shape[2], n // NC

    def stacked(source, first, size):
        rows = slice(first, first + size)
        return [ref[source, t, rows] for t in range(n_z) for ref in images]

    if not last:
        pixel = start_ref[0] + lax.broadcasted_iota(jnp.int32, (slab, half), 0)
        freq2 = (pixel.astype(jnp.float32) + 0.5) * (1.0 / width)
    for i, source in enumerate(sources):
        post = jnp.concatenate([posts[i][t] for t in range(n_z)], axis=1)
        for c in range(3):
            if c < 2:
                image = jnp.concatenate(stacked(source, c * half, half), axis=0)
                total = jnp.dot(post, image, preferred_element_type=jnp.float32)
            elif last:
                total = dot_nt(post, squares_ref[i])
            else:
                total = dot_nt(post, squares_of(stacked(source, n, TERM_ROWS), freq2))
            if i > 0:
                total += out_ref[c]
            elif last:
                total += before_ref[c]
            out_ref[c] = total
    for i, source in enumerate(ahead):
        squares_ref[i] = squares_of(stacked(source, n, TERM_ROWS), freq2)


def back_project(start, width, sources, posts, images, ahead=(), before=()):
    n_z, rows, n = posts[0].shape
    slab = images[0].shape[3]
    in_vmem = pl.BlockSpec(memory_space=pltpu.VMEM)
    out_shape = [jax.ShapeDtypeStruct((3, rows, slab), jnp.float32)]
    if ahead:
        out_shape.append(jax.ShapeDtypeStruct((len(ahead), slab, n_z * n), jnp.bfloat16))
    return pl.pallas_call(
        functools.partial(back_kernel, sources, ahead, width),
        in_specs=[pl.BlockSpec(memory_space=pltpu.SMEM)]
        + [in_vmem] * (len(sources) + 2 + len(before)),
        out_specs=[in_vmem] * len(out_shape),
        out_shape=out_shape,
        cost_estimate=SMALL_COST,
        compiler_params=pltpu.CompilerParams(vmem_limit_bytes=SMALL_VMEM),
        interpret=INTERPRET,
        name="back_project",
    )(start[None], *posts, *images, *before)


def exchange(copies, axis, groups=None):
    return lax.all_to_all(copies, axis, 0, 0, axis_index_groups=groups)


def copies_of(value, size):
    return jnp.broadcast_to(value[None], (size,) + value.shape)


def on_device(
    images, projections, defocus, inv_sigma2, log_prior, row_class, pose_block, significant
):
    _, n, width = images.shape
    _, rows, slab = projections.shape
    half = n // NC
    group, pose = lax.axis_index("grp"), lax.axis_index("pose")
    x = group >> 2
    y, zl, core = pose >> 3, (pose >> 1) & 3, pose & 1

    z_groups = [[a * NZH + b for b in range(NZH)] for a in range(NX)]
    x_groups = [[a * NZH + b for a in range(NX)] for b in range(NZH)]
    y_groups = [
        [(a * NZL + b) * NC + c for a in range(NY)] for b in range(NZL) for c in range(NC)
    ]
    with jax.named_scope("gather_projections"):
        proj_z = lax.all_gather(projections, "grp", axis=0, axis_index_groups=z_groups)
        proj_z, defocus = lax.optimization_barrier((proj_z, defocus))
        proj = lax.all_gather(proj_z, "grp", axis=0, axis_index_groups=x_groups)

    with jax.named_scope("exchange_images"):
        target = (((x + y) & 3) << 2) + zl
        cut = lax.dynamic_slice(images, (0, core * half, target * slab), (2, half, slab))
        part_defocus = lax.dynamic_slice(defocus, (core * half,), (half,))
        pixel = (target * slab + jnp.arange(slab)).astype(jnp.float32)
        contrast = -jnp.sin(part_defocus[:, None] * ((pixel + 0.5) / width)[None, :] + 0.1)
        cut = (cut.astype(jnp.float32) * contrast[None]).astype(jnp.bfloat16)
        terms = jnp.pad(defocus_terms(part_defocus), ((0, TERM_ROWS - 3), (0, slab - half)))
        share = jnp.concatenate([cut.reshape(2 * half, slab), terms], axis=0)
        share = lax.ppermute(share, ("grp", "pose"), share_pairs())

    with jax.named_scope("weights"):
        weighted, noise, part = weight_images(x, images, defocus, inv_sigma2, proj_z)
        class_match = row_class[:, None] == jnp.arange(log_prior.shape[0])[None, :]
        prior_rows = jnp.sum(jnp.where(class_match, log_prior[None, :], 0.0), axis=1)
        block_table = pose_block[:, None] == jnp.arange(significant.shape[1])[None, :]
        hits = jnp.einsum(
            "rb,ib->ri",
            block_table.astype(jnp.bfloat16),
            significant.astype(jnp.bfloat16),
            preferred_element_type=jnp.float32,
        )
        bias = jnp.where(hits > 0.5, prior_rows[:, None], jnp.float32(NEG_FILL))

    with jax.named_scope("gather_images"):
        share, part, bias = lax.optimization_barrier((share, part, bias))
        turned = copies_of(share, NZL)
        for d in (1, 2, 3):
            block = lax.ppermute(share, "pose", pose_shift(0, d, 0))
            turned = lax.dynamic_update_slice_in_dim(turned, block[None], (zl - d) & 3, 0)
        turned, proj = lax.optimization_barrier((turned, proj))
        own = lax.all_gather(turned, "pose", axis=0, axis_index_groups=y_groups)

    with jax.named_scope("scores"):
        scores, log_sum = score(x, proj, weighted, noise, part, bias, NY * NZL * NC)

    with jax.named_scope("softmax"):
        posteriors, post_bf = posterior(core, scores, exchange(log_sum, "pose"))

    with jax.named_scope("gather_posteriors"):
        post = [lax.all_gather(post_bf, "grp", axis=0, axis_index_groups=z_groups)] + [None] * 3
        for d in (1, 2, 3):
            post[d] = lax.ppermute(post[0], "grp", grp_shift(d))
        post[0], own = lax.optimization_barrier((post[0], own))
        other = lax.ppermute(own, "pose", pose_shift(0, 0, 1))

    with jax.named_scope("back_project"):
        start = group * slab
        near, far, stacks = (0,), (1, 2, 3), (own, other)
        before = back_project(start, width, near, [post[d] for d in near], stacks, ahead=far)
        (back_proj,) = back_project(start, width, far, [post[d] for d in far], stacks, before=before)
    return (posteriors, back_proj)


def solution(mesh):
    placed = (
        P(None, "grp", None),
        P(None, "pose", "grp"),
        P("grp"),
        P(),
        P(),
        P("pose"),
        P("pose"),
        P("grp", None),
    )
    return jax.shard_map(
        on_device,
        mesh=mesh,
        in_specs=placed,
        out_specs=(P("grp", "pose"), P(None, "pose", "grp")),
        check_vma=False,
    )
```
